32 devices in a mesh: rows: 4 (over y, x), pts: 8 (over z, core).
Axes of the slice: x: 2, y: 2, z: 4, core: 2. Of those that a mesh axis runs over, the one named last changes fastest.
Arguments:
- env_desc: bfloat16 [2048, 1024], P('rows', 'pts'), may hold values from -6 to 6
- point_desc: bfloat16 [16384, 1024], P('pts', 'rows'), may hold values from -6 to 6
- pool_index: int32 [1024, 4], P('rows'), may hold values from 0 to 511
- pool_count: int32 [1024], P('rows'), may hold values from 1 to 4
- pool_weight: float32 [1024, 4], P('rows'), may hold values from -3 to 3
- row_dest: int32 [1024], P('rows'), may hold values from -1 to 511, as said below
Outputs:
- design: float32 [512, 16384], P('rows', 'pts')
- gram: float32 [16384, 16384], P('rows', 'pts')
The draws below stay inside these ranges and needn't reach their ends.
Inputs may be any that keep to these rules, and one draw needn't show every extreme that they name: Slot s pools environments (s // 256) * 512 + pool_index[s, j] of its own structure group. Slot s pools its first pool_count[s] entries. `row_dest`: -1 marks an empty slot; every row 0 .. 511 is named by exactly one slot; the slots of one structure group (aligned blocks of 256 slots) name at most 64 rows of any aligned block of 128 rows, and in every draw some structure group names exactly 64 rows of every such block.
All inputs are finite; a program needn't handle non-finite values.
Results may differ from the reference program's by a relative error of at most 0.0003.
Values may be sent and summed in bfloat16 or wider, within the bound.
No kernel may reach another device: no remote copies, remote signals or barrier semaphores. Data moves between devices by JAX's collectives and lax.ppermute only.
A program may use at most 128 MiB of HBM per device.

```python
import jax
import jax.numpy as jnp
from jax import lax

W = 1024
PTS = 16384
POOL = 4
E_DEV = 512
ROW_CAP = 256
R_BAL = 128
ENVS = 2048
SLOTS = 1024
ROWS = 512
N_ROWS = 4
N_PTS = 8


def draw_row_dest(key, part):
    groups = N_ROWS
    subkeys = jax.random.split(jax.random.fold_in(key, 11), 4)
    half_count = groups // 2
    shifts = jax.random.randint(subkeys[0], (half_count,), -R_BAL, R_BAL + 1).astype(jnp.int32)
    shifts = shifts.at[0].set(R_BAL)
    changes = jnp.concatenate([shifts, -shifts])
    device_order = jax.random.permutation(subkeys[1], groups)
    live_counts = (R_BAL + changes)[device_order].astype(jnp.int32)
    first_rows = jnp.cumsum(live_counts) - live_counts
    slot_orders = jax.vmap(lambda subkey: jax.random.permutation(subkey, ROW_CAP))(jax.random.split(subkeys[2], groups))
    slot_rank = jnp.argsort(slot_orders, axis=1).astype(jnp.int32)
    live_slot = slot_rank < live_counts[:, None]
    global_row = first_rows[:, None] + slot_rank
    dest_group = global_row % groups
    within = jnp.clip(global_row // groups, 0, R_BAL - 1)
    positions = jax.vmap(lambda subkey: jax.random.permutation(subkey, R_BAL))(jax.random.split(subkeys[3], groups)).astype(jnp.int32)
    position = positions[dest_group, within]
    result = jnp.where(live_slot, dest_group * R_BAL + position, -1)
    return result.reshape(SLOTS).astype(jnp.int32)


def set_ends(drawn, own_key, low, largest):
    longest = drawn.shape.index(max(drawn.shape))
    spots = []
    for shift in (0, 1):
        where = [jax.random.randint(jax.random.fold_in(own_key, axis), (), 0, length) for axis, length in enumerate(drawn.shape)]
        where[longest] = (where[longest] + shift) % drawn.shape[longest]
        spots.append(tuple(where))
    return drawn.at[spots[0]].set(low).at[spots[1]].set(largest)


def steps_of(rng, extent, pieces, low, high):
    factor_of = 1.0
    for dim, parts in pieces:
        steps = jax.random.uniform(jax.random.fold_in(jax.random.fold_in(rng, 6), dim), (parts,), jnp.float32, low / len(pieces), high / len(pieces))
        factor_of = factor_of * jnp.repeat(jnp.exp(steps), extent[dim] // parts).reshape((-1,) + (1,) * (len(extent) - 1 - dim))
    return factor_of


def normal_values(stream_key, shape, scale, most, shards=(), held_as=jnp.bfloat16):
    gain = steps_of(stream_key, shape, shards, -0.22, 0.18) if shards else 1.0
    drawn = jax.random.normal(stream_key, shape, jnp.float32) * scale * gain
    return jnp.minimum(jnp.maximum(drawn, -most), most).astype(held_as)


def setup_inputs(seed: int = 0) -> dict:
    arg_keys = jax.random.split(jax.random.key(seed), 7)
    return {
        "env_desc": normal_values(arg_keys[0], (ENVS, W), 1.0, 6.0, ((0, 4), (1, 8))),
        "point_desc": normal_values(arg_keys[1], (PTS, W), 1.0, 6.0, ((0, 8), (1, 4))),
        "pool_index": set_ends(jax.random.randint(arg_keys[2], (SLOTS, POOL), 0, E_DEV), jax.random.fold_in(arg_keys[2], 1), 0, E_DEV - 1).astype(jnp.int32),
        "pool_count": set_ends(jax.random.randint(arg_keys[3], (SLOTS,), 1, POOL + 1), jax.random.fold_in(arg_keys[3], 1), 1, POOL).astype(jnp.int32),
        "pool_weight": normal_values(arg_keys[4], (SLOTS, POOL), 0.5, 3.0, ((0, 4),), jnp.float32),
        "row_dest": draw_row_dest(jax.random.fold_in(arg_keys[6], 71), 0),
    }


damping = 0.5


def kernel_values(left, right):
    products = lax.dot_general(left, right, (((1,), (1,)), ((), ())), preferred_element_type=jnp.float32)
    scaled = products * (left.shape[1] ** -0.5)
    squared = scaled * scaled
    return 0.25 * squared * squared


def live_weights(pool_count, pool_weight):
    members = jnp.arange(pool_weight.shape[1], dtype=jnp.int32)
    return jnp.where(members[None, :] < pool_count[:, None], pool_weight, 0.0)


def pool_rows(kernel_table, env_index, weights_live):
    pooled = jnp.zeros((env_index.shape[0], kernel_table.shape[1]), kernel_table.dtype)
    for member in range(env_index.shape[1]):
        pooled = pooled + weights_live[:, member:member + 1] * kernel_table[env_index[:, member]]
    return pooled


def reference(env_desc, point_desc, pool_index, pool_count, pool_weight, row_dest):
    group_start = (jnp.arange(SLOTS, dtype=jnp.int32) // ROW_CAP) * E_DEV
    env_index = pool_index + group_start[:, None]
    weights_live = live_weights(pool_count, pool_weight)
    point_blocks = point_desc.reshape(N_PTS, PTS // N_PTS, W)

    def one_block(points):
        return pool_rows(kernel_values(env_desc, points), env_index, weights_live)

    slot_rows = lax.map(one_block, point_blocks)
    slot_rows = jnp.transpose(slot_rows, (1, 0, 2)).reshape(SLOTS, PTS)
    target = jnp.where(row_dest >= 0, row_dest, ROWS)
    design = jnp.zeros((ROWS, PTS), jnp.float32).at[target].set(slot_rows, mode="drop")
    gram_full = lax.dot_general(design, design, (((0,), (0,)), ((), ())), precision=lax.Precision.HIGHEST, preferred_element_type=jnp.float32)
    gram_full = gram_full * (1.0 / ROWS)
    diagonal = jnp.arange(PTS, dtype=jnp.int32)
    gram_full = gram_full.at[diagonal, diagonal].add(damping)
    return design, gram_full
```

```python
import functools

import jax
import jax.numpy as jnp
from jax import lax
from jax.experimental import pallas as pl
from jax.experimental.pallas import tpu as pltpu
from jax.sharding import PartitionSpec as P

damping = 0.5
CODE_TOP = 32700.0
BOTH = ("rows", "pts")
MIB = 1 << 20
F32 = jnp.float32
BF16 = jnp.bfloat16


def from_root(value, axis, source):
    kept = jnp.where(lax.axis_index(axis) == source, value, 0).astype(value.dtype)
    return lax.psum(kept, axis)


def kernel_values(left, right):
    products = lax.dot_general(
        left, right, (((1,), (1,)), ((), ())), preferred_element_type=jnp.float32
    )
    scaled = products * left.shape[1] ** (-0.5)
    squared = scaled * scaled
    return 0.25 * squared * squared


def live_weights(pool_count, pool_weight):
    members = jnp.arange(pool_weight.shape[1], dtype=jnp.int32)
    return jnp.where(members[None, :] < pool_count[:, None], pool_weight, 0.0)


def pool_rows(kernel_table, env_index, weights_live):
    pooled = jnp.zeros((env_index.shape[0], kernel_table.shape[1]), jnp.float32)
    for member in range(env_index.shape[1]):
        pooled = pooled + weights_live[:, member : member + 1] * kernel_table[env_index[:, member]]
    return pooled


def on_any_device(env_desc, point_desc, pool_index, pool_count, pool_weight, row_dest):
    groups = lax.axis_size("rows")
    slot_total = pool_index.shape[0]
    balanced = slot_total // 2
    slot_share = slot_total // groups
    points = lax.all_gather(point_desc, "rows", axis=1, tiled=True)
    width_pts = points.shape[0]
    weights_live = live_weights(pool_count, pool_weight)
    live_slot = row_dest >= 0
    owner_group = jnp.where(live_slot, row_dest // balanced, groups)
    within = jnp.where(live_slot, row_dest % balanced, balanced)
    owner_table = (owner_group[:, None] == jnp.arange(groups, dtype=jnp.int32)[None, :]).astype(
        jnp.int32
    )
    earlier = jnp.cumsum(owner_table, axis=0) - owner_table
    slot_rank = jnp.sum(earlier * owner_table, axis=1)
    outbox_place = (
        jnp.full((groups, slot_share), balanced, jnp.int32)
        .at[owner_group, slot_rank]
        .set(within, mode="drop")
    )
    features = lax.all_gather(env_desc, "pts", axis=1, tiled=True)
    slot_rows = pool_rows(kernel_values(features, points), pool_index, weights_live)
    outbox = (
        jnp.zeros((groups, slot_share, width_pts), jnp.float32)
        .at[owner_group, slot_rank]
        .set(slot_rows, mode="drop")
    )
    inbox_rows, inbox_place = (
        lax.all_to_all(outbox, "rows", split_axis=0, concat_axis=0, tiled=True),
        lax.all_to_all(outbox_place, "rows", split_axis=0, concat_axis=0, tiled=True),
    )
    design = (
        jnp.zeros((balanced, width_pts), jnp.float32)
        .at[inbox_place.reshape(-1)]
        .set(inbox_rows.reshape(-1, width_pts), mode="drop")
    )
    all_rows = lax.all_gather(design, "rows", axis=0, tiled=True)
    per_group = lax.axis_size("pts") // groups
    row_group = lax.axis_index("rows")
    pieces = []
    for part_index in range(per_group):
        diagonal_panel = from_root(all_rows, "pts", row_group * per_group + part_index)
        pieces.append(
            lax.dot_general(
                diagonal_panel,
                all_rows,
                (((0,), (0,)), ((), ())),
                precision=lax.Precision.HIGHEST,
                preferred_element_type=jnp.float32,
            )
        )
    gram_tile = jnp.concatenate(pieces, axis=0) * (1.0 / all_rows.shape[0])
    tile_rows = gram_tile.shape[0]
    row_ids = row_group * tile_rows + jnp.arange(tile_rows, dtype=jnp.int32)
    col_ids = lax.axis_index("pts") * width_pts + jnp.arange(width_pts, dtype=jnp.int32)
    gram_tile = gram_tile + jnp.where(row_ids[:, None] == col_ids[None, :], damping, 0.0)
    return (design, gram_tile)


def dot_nn(a, b):
    return lax.dot_general(a, b, (((1,), (0,)), ((), ())), preferred_element_type=F32)


def dot_nt(a, b):
    return lax.dot_general(a, b, (((1,), (1,)), ((), ())), preferred_element_type=F32)


def split(value):
    high = value.astype(BF16)
    return high, (value - high.astype(F32)).astype(BF16)


def encode(value, code_ref):
    n = value.shape[0]
    size = jnp.abs(value)
    top = jnp.maximum(jnp.max(size, axis=0, keepdims=True), 1e-30)
    exponent = jnp.ceil(jnp.log(top) * 1.4426950408889634)
    root = jnp.sqrt(size * jnp.exp2(-exponent))
    code = jnp.minimum(root * CODE_TOP + 0.5, 32767.0).astype(jnp.int32)
    code_ref[pl.ds(0, n), :] = jnp.where(value < 0, -code, code).astype(jnp.int16)
    pad = code_ref.shape[0] - n
    code_ref[pl.ds(n, pad), :] = jnp.broadcast_to(
        exponent.astype(jnp.int32), (pad, value.shape[1])
    ).astype(jnp.int16)


def lane_scale(exponent_rows, extra):
    exponent = exponent_rows.astype(jnp.int32).astype(F32)[0:1, :]
    return jnp.exp2(exponent) * (extra / (CODE_TOP * CODE_TOP))


def decode(codes, scale):
    root = codes.astype(jnp.int32).astype(F32)
    return root * jnp.abs(root) * scale


def weights_kernel(table_ref, high_ref, low_ref):
    groups, rows, envs = high_ref.shape
    table = table_ref[...]
    slots = table.shape[0]
    row_id = lax.broadcasted_iota(jnp.int32, (slots, rows), 1).astype(F32)
    chosen = jnp.where(table[:, 8:9] == row_id, 1.0, 0.0)
    by_row = lax.dot_general(
        chosen,
        table,
        (((0,), (0,)), ((), ())),
        precision=lax.Precision.HIGHEST,
        preferred_element_type=F32,
    )
    env_id = lax.broadcasted_iota(jnp.int32, (rows, envs), 1).astype(F32)
    index = jnp.floor(by_row + 0.5)
    for group in range(groups):
        ids = env_id + float(group * envs)
        total = jnp.zeros((rows, envs), F32)
        for member in range(4):
            total = total + jnp.where(
                index[:, member : member + 1] == ids, by_row[:, 4 + member : 5 + member], 0.0
            )
        high, low = split(total)
        high_ref[group] = high
        low_ref[group] = low


def design_kernel(
    at_ref,
    own0,
    own1,
    own2,
    own3,
    swap0,
    swap1,
    swap2,
    swap3,
    cols_ref,
    pan0,
    pan1,
    pan2,
    pan3,
    high_ref,
    low_ref,
    cols_code,
    panel_code,
    rows_out,
    env,
    pts,
    cols_sum,
    panel_sum,
):
    q, z, core = at_ref[0], at_ref[1], at_ref[2]
    n_pts = cols_ref.shape[1]
    comps = cols_ref.shape[2]
    part = own0.shape[2]
    tile = 256
    for j in range(4):
        pts[pl.ds(0, n_pts), pl.ds(j * comps, comps)] = cols_ref[j]
    for t, ref in enumerate((pan0, pan1, pan2, pan3)):
        at = pl.multiple_of(jnp.bitwise_xor(z, t) * comps, comps)
        pts[pl.ds(n_pts, n_pts), pl.ds(at, comps)] = ref[...]
    for d, (own, swap) in enumerate(
        zip((own0, own1, own2, own3), (swap0, swap1, swap2, swap3))
    ):
        group = jnp.bitwise_xor(q, d)
        for r in range(4):
            base = jnp.bitwise_xor(z, r) * comps
            mine = pl.multiple_of(base + core * part, part)
            other = pl.multiple_of(base + (1 - core) * part, part)
            env[:, pl.ds(mine, part)] = own[r]
            env[:, pl.ds(other, part)] = swap[r]
        features = env[...]
        high, low = high_ref[group], low_ref[group]
        scale = env.shape[1] ** (-0.5)
        for i in range(n_pts // tile):
            lanes = pl.ds(i * tile, tile)
            s = dot_nt(features, pts[lanes, :]) * scale
            s = s * s
            k_high, k_low = split(0.25 * s * s)
            part_sum = dot_nn(high, k_high) + dot_nn(high, k_low) + dot_nn(low, k_high)
            cols_sum[:, lanes] = part_sum if d == 0 else cols_sum[:, lanes] + part_sum
        for i in range(n_pts // tile):
            rows = pl.ds(i * tile, tile)
            s = dot_nt(pts[pl.ds(n_pts + i * tile, tile), :], features) * scale
            s = s * s
            k_high, k_low = split(0.25 * s * s)
            part_sum = dot_nt(k_high, high) + dot_nt(k_low, high) + dot_nt(k_high, low)
            panel_sum[rows, :] = part_sum if d == 0 else panel_sum[rows, :] + part_sum
    encode(cols_sum[...], cols_code)
    encode(panel_sum[...], panel_code)
    share = rows_out.shape[0]
    rows_out[...] = cols_sum[pl.ds(pl.multiple_of(q * share, share), share), :]


def columns_kernel(at_ref, codes_ref, rows_ref, triple_ref, design_ref):
    n = pl.program_id(0)
    q = at_ref[0]
    rows = triple_ref.shape[0] // 3
    share = design_ref.shape[0]
    scale = lane_scale(codes_ref[0, pl.ds(rows, 16), :], 1.0)
    value = decode(codes_ref[0, pl.ds(0, rows), :], scale)
    high, low = split(value)
    triple_ref[pl.ds(0, rows), :] = high
    triple_ref[pl.ds(rows, rows), :] = high
    triple_ref[pl.ds(2 * rows, rows), :] = low

    @pl.when(n == q)
    def _():
        design_ref[...] = rows_ref[...]

    @pl.when(n != q)
    def _():
        start = pl.multiple_of(q * share, share)
        design_ref[...] = decode(codes_ref[0, pl.ds(start, share), :], scale)


def gram_kernel(at_ref, own_ref, swap_ref, triple_ref, *refs):
    out_ref, left = refs[-2], refs[-1]
    j = pl.program_id(0)
    k, z, core, source = at_ref[0], at_ref[1], at_ref[2], at_ref[3]
    n_pts = out_ref.shape[1]
    rows = own_ref.shape[1]

    @pl.when(j == 0)
    def _():
        for ref, side in ((own_ref, core), (swap_ref, 1 - core)):
            scale = lane_scale(ref[pl.ds(n_pts, 16), :], 1.0 / rows)
            high, low = split(decode(ref[pl.ds(0, n_pts), :], scale))
            left[side, :, pl.ds(0, rows)] = high
            left[side, :, pl.ds(rows, rows)] = low
            left[side, :, pl.ds(2 * rows, rows)] = high

    for side in range(2):
        out_ref[side] = dot_nn(left[side], triple_ref[...])

    @pl.when((k == z) & (j == source))
    def _():
        eye = lax.broadcasted_iota(jnp.int32, out_ref.shape[1:], 0) == lax.broadcasted_iota(
            jnp.int32, out_ref.shape[1:], 1
        )
        out_ref[core] = out_ref[core] + jnp.where(eye, damping, 0.0)


def whole(shape):
    return pl.BlockSpec(shape, lambda *_: (0,) * len(shape))


def on_device(env_desc, point_desc, pool_index, pool_count, pool_weight, row_dest):
    groups, planes = 4, 4
    q = lax.axis_index("rows")
    p = lax.axis_index("pts")
    z, core = p // 2, p % 2
    at = jnp.stack([q, z, core, z]).astype(jnp.int32)
    n_rows = pool_index.shape[0] * groups // 2
    envs, part = env_desc.shape
    n_pts = point_desc.shape[0] // planes
    comps = point_desc.shape[1]
    n_pool = pool_index.shape[1]
    pad = n_rows + 16

    def permutation(to):
        return [
            (r * 8 + s, to(r, s // 2, s % 2)[0] * 8 + to(r, s // 2, s % 2)[1] * 2 + to(r, s // 2, s % 2)[2])
            for r in range(groups)
            for s in range(planes * 2)
        ]

    def moved(value, to):
        return lax.ppermute(value, BOTH, permutation(to))

    along_x = lambda r, h, c: (r ^ 1, h, c)
    along_y = lambda r, h, c: (r ^ 2, h, c)
    to_core = lambda r, h, c: (r, h, 1 - c)
    ring = (1, 3, 0, 2)
    along_z = lambda r, h, c: (r, ring[h], c)

    pair = jnp.stack([env_desc, moved(env_desc, lambda r, h, c: (r, h ^ 1, c))])
    own = jnp.concatenate([pair, moved(pair, lambda r, h, c: (r, h ^ 2, c))])

    quarters = point_desc.reshape(planes, n_pts, comps)
    cols_pts = lax.all_to_all(quarters, "rows", 0, 0, tiled=True)
    panel_pts = [
        moved(
            lax.dynamic_index_in_dim(quarters, q ^ t, 0, keepdims=False),
            lambda r, h, c, t=t: (h, r ^ t, c),
        )
        for t in range(planes)
    ]

    members = jnp.arange(n_pool, dtype=jnp.int32)
    live = jnp.where(members[None, :] < pool_count[:, None], pool_weight, 0.0)
    table = jnp.concatenate(
        [
            (pool_index + q * envs).astype(F32),
            live,
            row_dest[:, None].astype(F32),
            jnp.zeros((pool_index.shape[0], 7), F32),
        ],
        axis=1,
    )
    table = lax.all_gather(table, "rows", axis=0, tiled=True)
    high, low = pl.pallas_call(
        weights_kernel,
        out_shape=[jax.ShapeDtypeStruct((groups, n_rows, envs), BF16)] * 2,
        compiler_params=pltpu.CompilerParams(vmem_limit_bytes=48 * MIB),
        name="pool_weights",
    )(table)

    from_x, from_y = moved(own, along_x), moved(own, along_y)
    from_xy = jnp.concatenate([moved(from_x[:2], along_y), moved(from_y[2:], along_x)])
    mine = (own, from_x, from_y, from_xy)
    swapped = [moved(e, to_core) for e in mine]

    env_spec = whole((planes, envs, part))
    cols_code, panel_code, own_rows = pl.pallas_call(
        design_kernel,
        grid_spec=pltpu.PrefetchScalarGridSpec(
            num_scalar_prefetch=1,
            grid=(1,),
            in_specs=[env_spec] * 8
            + [whole((groups, n_pts, comps))]
            + [whole((n_pts, comps))] * 4
            + [whole((groups, n_rows, envs))] * 2,
            out_specs=[
                whole((pad, n_pts)),
                whole((n_pts + 16, n_rows)),
                whole((n_rows // groups, n_pts)),
            ],
            scratch_shapes=[
                pltpu.VMEM((envs, groups * comps), BF16),
                pltpu.VMEM((2 * n_pts, groups * comps), BF16),
                pltpu.VMEM((n_rows, n_pts), F32),
                pltpu.VMEM((n_pts, n_rows), F32),
            ],
        ),
        out_shape=[
            jax.ShapeDtypeStruct((pad, n_pts), jnp.int16),
            jax.ShapeDtypeStruct((n_pts + 16, n_rows), jnp.int16),
            jax.ShapeDtypeStruct((n_rows // groups, n_pts), F32),
        ],
        compiler_params=pltpu.CompilerParams(vmem_limit_bytes=56 * MIB),
        name="design_values",
    )(at, *mine, *swapped, cols_pts, *panel_pts, high, low)

    codes = lax.all_to_all(
        jnp.broadcast_to(cols_code[None], (groups, pad, n_pts)), "rows", 0, 0, tiled=True
    )
    width = groups * n_pts
    triple, design = pl.pallas_call(
        columns_kernel,
        grid_spec=pltpu.PrefetchScalarGridSpec(
            num_scalar_prefetch=1,
            grid=(groups,),
            in_specs=[
                pl.BlockSpec((1, pad, n_pts), lambda n, _: (n, 0, 0)),
                whole((n_rows // groups, n_pts)),
            ],
            out_specs=[
                pl.BlockSpec((3 * n_rows, n_pts), lambda n, _: (0, n)),
                pl.BlockSpec((n_rows // groups, n_pts), lambda n, _: (0, n)),
            ],
        ),
        out_shape=[
            jax.ShapeDtypeStruct((3 * n_rows, width), BF16),
            jax.ShapeDtypeStruct((n_rows // groups, width), F32),
        ],
        compiler_params=pltpu.CompilerParams(vmem_limit_bytes=48 * MIB),
        name="columns",
    )(at, codes, own_rows)

    held, source = panel_code, z
    gram = None
    for step in range(planes):
        other = moved(held, to_core)
        passed = moved(held, along_z) if step < planes - 1 else None
        in_specs = [
            whole((n_pts + 16, n_rows)),
            whole((n_pts + 16, n_rows)),
            pl.BlockSpec((3 * n_rows, n_pts), lambda j, _: (0, j)),
        ]
        operands = [jnp.stack([q, z, core, source]).astype(jnp.int32), held, other, triple]
        if gram is not None:
            in_specs.append(pl.BlockSpec(memory_space=pl.ANY))
            operands.append(gram)
        gram = pl.pallas_call(
            gram_kernel,
            grid_spec=pltpu.PrefetchScalarGridSpec(
                num_scalar_prefetch=1,
                grid=(groups,),
                in_specs=in_specs,
                out_specs=pl.BlockSpec((2, n_pts, n_pts), lambda j, s: (0, s[3], j)),
                scratch_shapes=[pltpu.VMEM((2, n_pts, 3 * n_rows), BF16)],
            ),
            out_shape=jax.ShapeDtypeStruct((2, planes * n_pts, width), F32),
            input_output_aliases={} if gram is None else {4: 0},
            compiler_params=pltpu.CompilerParams(vmem_limit_bytes=48 * MIB),
            name="gram_rows",
        )(*operands)
        held = passed
        source = jnp.take(jnp.array([2, 0, 3, 1], jnp.int32), source)
    return design, gram.reshape(2 * planes * n_pts, width)


def solution(mesh):
    in_specs = (
        P("rows", "pts"),
        P("pts", "rows"),
        P("rows", None),
        P("rows"),
        P("rows", None),
        P("rows"),
    )
    out_specs = (P("rows", "pts"), P("rows", "pts"))
    body = on_device if dict(mesh.shape) == {"rows": 4, "pts": 8} else on_any_device
    return jax.shard_map(body, mesh=mesh, in_specs=in_specs, out_specs=out_specs, check_vma=False)
```

```python
import functools

import jax
import jax.numpy as jnp
from jax import lax
from jax.experimental import pallas as pl
from jax.experimental.pallas import tpu as pltpu
from jax.sharding import PartitionSpec as P

damping = 0.5
CODE_TOP = 32700.0
BOTH = ("rows", "pts")
MIB = 1 << 20
VMEM_LIMIT = 63 * MIB
F32 = jnp.float32
BF16 = jnp.bfloat16


def from_root(value, axis, source):
    kept = jnp.where(lax.axis_index(axis) == source, value, 0).astype(value.dtype)
    return lax.psum(kept, axis)


def kernel_values(left, right):
    products = lax.dot_general(
        left, right, (((1,), (1,)), ((), ())), preferred_element_type=jnp.float32
    )
    scaled = products * left.shape[1] ** (-0.5)
    squared = scaled * scaled
    return 0.25 * squared * squared


def live_weights(pool_count, pool_weight):
    members = jnp.arange(pool_weight.shape[1], dtype=jnp.int32)
    return jnp.where(members[None, :] < pool_count[:, None], pool_weight, 0.0)


def pool_rows(kernel_table, env_index, weights_live):
    pooled = jnp.zeros((env_index.shape[0], kernel_table.shape[1]), jnp.float32)
    for member in range(env_index.shape[1]):
        pooled = pooled + weights_live[:, member : member + 1] * kernel_table[env_index[:, member]]
    return pooled


def on_any_device(env_desc, point_desc, pool_index, pool_count, pool_weight, row_dest):
    groups = lax.axis_size("rows")
    slot_total = pool_index.shape[0]
    balanced = slot_total // 2
    slot_share = slot_total // groups
    points = lax.all_gather(point_desc, "rows", axis=1, tiled=True)
    width_pts = points.shape[0]
    weights_live = live_weights(pool_count, pool_weight)
    live_slot = row_dest >= 0
    owner_group = jnp.where(live_slot, row_dest // balanced, groups)
    within = jnp.where(live_slot, row_dest % balanced, balanced)
    owner_table = (owner_group[:, None] == jnp.arange(groups, dtype=jnp.int32)[None, :]).astype(
        jnp.int32
    )
    earlier = jnp.cumsum(owner_table, axis=0) - owner_table
    slot_rank = jnp.sum(earlier * owner_table, axis=1)
    outbox_place = (
        jnp.full((groups, slot_share), balanced, jnp.int32)
        .at[owner_group, slot_rank]
        .set(within, mode="drop")
    )
    features = lax.all_gather(env_desc, "pts", axis=1, tiled=True)
    slot_rows = pool_rows(kernel_values(features, points), pool_index, weights_live)
    outbox = (
        jnp.zeros((groups, slot_share, width_pts), jnp.float32)
        .at[owner_group, slot_rank]
        .set(slot_rows, mode="drop")
    )
    inbox_rows, inbox_place = (
        lax.all_to_all(outbox, "rows", split_axis=0, concat_axis=0, tiled=True),
        lax.all_to_all(outbox_place, "rows", split_axis=0, concat_axis=0, tiled=True),
    )
    design = (
        jnp.zeros((balanced, width_pts), jnp.float32)
        .at[inbox_place.reshape(-1)]
        .set(inbox_rows.reshape(-1, width_pts), mode="drop")
    )
    all_rows = lax.all_gather(design, "rows", axis=0, tiled=True)
    per_group = lax.axis_size("pts") // groups
    row_group = lax.axis_index("rows")
    pieces = []
    for part_index in range(per_group):
        diagonal_panel = from_root(all_rows, "pts", row_group * per_group + part_index)
        pieces.append(
            lax.dot_general(
                diagonal_panel,
                all_rows,
                (((0,), (0,)), ((), ())),
                precision=lax.Precision.HIGHEST,
                preferred_element_type=jnp.float32,
            )
        )
    gram_tile = jnp.concatenate(pieces, axis=0) * (1.0 / all_rows.shape[0])
    tile_rows = gram_tile.shape[0]
    row_ids = row_group * tile_rows + jnp.arange(tile_rows, dtype=jnp.int32)
    col_ids = lax.axis_index("pts") * width_pts + jnp.arange(width_pts, dtype=jnp.int32)
    gram_tile = gram_tile + jnp.where(row_ids[:, None] == col_ids[None, :], damping, 0.0)
    return (design, gram_tile)


def dot_nn(a, b):
    return lax.dot_general(a, b, (((1,), (0,)), ((), ())), preferred_element_type=F32)


def dot_nt(a, b):
    return lax.dot_general(a, b, (((1,), (1,)), ((), ())), preferred_element_type=F32)


def split(value):
    high = value.astype(BF16)
    return high, (value - high.astype(F32)).astype(BF16)


def encode(value, code_ref):
    n = value.shape[0]
    size = jnp.abs(value)
    top = jnp.maximum(jnp.max(size, axis=0, keepdims=True), 1e-30)
    exponent = jnp.ceil(jnp.log(top) * 1.4426950408889634)
    root = jnp.sqrt(size * jnp.exp2(-exponent))
    code = jnp.minimum(root * CODE_TOP + 0.5, 32767.0).astype(jnp.int32)
    code_ref[pl.ds(0, n), :] = jnp.where(value < 0, -code, code).astype(jnp.int16)
    pad = code_ref.shape[0] - n
    code_ref[pl.ds(n, pad), :] = jnp.broadcast_to(
        exponent.astype(jnp.int32), (pad, value.shape[1])
    ).astype(jnp.int16)


def lane_scale(exponent_rows, extra):
    exponent = exponent_rows.astype(jnp.int32).astype(F32)[0:1, :]
    return jnp.exp2(exponent) * (extra / (CODE_TOP * CODE_TOP))


def decode(codes, scale):
    root = codes.astype(jnp.int32).astype(F32)
    return root * jnp.abs(root) * scale


def weights_kernel(table_ref, high_ref, low_ref):
    groups, rows, envs = high_ref.shape
    shares = []
    for g in range(groups):
        piece = table_ref[g].astype(F32)
        index = piece[0:4] * 256.0 + piece[4:8] + float(g * envs)
        weight = piece[8:12] + piece[12:16] + piece[16:20]
        place = piece[20:21] * 256.0 + piece[21:22] - 1.0
        shares.append(jnp.concatenate([index, weight, place], axis=0))
    table = jnp.concatenate(shares, axis=1)
    slots = table.shape[1]
    row_id = lax.broadcasted_iota(jnp.int32, (rows, slots), 0).astype(F32)
    chosen = jnp.where(table[8:9, :] == row_id, 1.0, 0.0)
    by_row = lax.dot_general(
        chosen,
        table,
        (((1,), (1,)), ((), ())),
        precision=lax.Precision.HIGHEST,
        preferred_element_type=F32,
    )
    env_id = lax.broadcasted_iota(jnp.int32, (rows, envs), 1).astype(F32)
    index = jnp.floor(by_row + 0.5)
    for group in range(groups):
        ids = env_id + float(group * envs)
        total = jnp.zeros((rows, envs), F32)
        for member in range(4):
            total = total + jnp.where(
                index[:, member : member + 1] == ids, by_row[:, 4 + member : 5 + member], 0.0
            )
        high, low = split(total)
        high_ref[group] = high
        low_ref[group] = low


def fourth_power(products, scale):
    s = products * scale
    s = s * s
    return split(0.25 * s * s)


def add_columns(features, weights, pts, total, first):
    high, low = weights[0], weights[1]
    k_high, k_low = fourth_power(dot_nt(features, pts[...]), features.shape[1] ** (-0.5))
    part = dot_nn(high, k_high) + dot_nn(high, k_low) + dot_nn(low, k_high)
    total[...] = part if first else total[...] + part


def add_panel(features, weights, pts, total, first):
    high, low = weights[0], weights[1]
    k_high, k_low = fourth_power(dot_nt(pts[...], features), features.shape[1] ** (-0.5))
    part = dot_nt(k_high, high) + dot_nt(k_low, high) + dot_nt(k_high, low)
    total[...] = part if first else total[...] + part


def started(copies):
    for copy in copies:
        copy.start()
    return copies


def waited(copies):
    for copy in copies:
        copy.wait()


def group_copies(at_ref, group, mine, swapped, high, low, env, weights, sems):
    z, core = at_ref[1], at_ref[2]
    part = mine.shape[3]
    out = []
    for side, ref in ((core, mine), (1 - core, swapped)):
        for r in range(4):
            at = pl.multiple_of((jnp.bitwise_xor(z, r) * 2 + side) * part, part)
            to = env.at[:, pl.ds(at, part)]
            out.append(pltpu.make_async_copy(ref.at[group, r], to, sems.at[len(out)]))
    for i, ref in enumerate((high, low)):
        out.append(pltpu.make_async_copy(ref.at[group], weights.at[i], sems.at[8 + i]))
    return out


def design_kernel(
    at_ref, mine, swapped, cols, pan0, pan1, pan2, pan3, high, low,
    cols_code, panel_code, rows_out,
    cols_pts, panel_pts, env, weights, cols_sum, panel_sum, point_sems, group_sems,
):
    q, z = at_ref[0], at_ref[1]
    n_pts, comps = pan0.shape
    points = []
    for j in range(4):
        to = cols_pts.at[:, pl.ds(j * comps, comps)]
        source = cols.at[j, pl.ds(0, n_pts)]
        points.append(pltpu.make_async_copy(source, to, point_sems.at[j]))
    started(points)
    copies = [
        group_copies(at_ref, d, mine, swapped, high, low, env.at[d], weights.at[d], group_sems.at[d])
        for d in range(4)
    ]
    started(copies[0])
    panel = []
    for t, ref in enumerate((pan0, pan1, pan2, pan3)):
        at = pl.multiple_of(jnp.bitwise_xor(z, t) * comps, comps)
        to = panel_pts.at[:, pl.ds(at, comps)]
        panel.append(pltpu.make_async_copy(ref, to, point_sems.at[4 + t]))
    started(panel)
    for d in range(1, 4):
        started(copies[d])
    waited(points)
    for d in range(4):
        waited(copies[d])
        add_columns(env[d], weights.at[d], cols_pts, cols_sum, d == 0)
        if d == 0:
            waited(panel)
        add_panel(env[d], weights.at[d], panel_pts, panel_sum, d == 0)
    encode(cols_sum[...], cols_code)
    share = rows_out.shape[0]
    rows_out[...] = cols_sum[pl.ds(pl.multiple_of(q * share, share), share), :]
    encode(panel_sum[...], panel_code)


def value_pair(codes, scale, out):
    rows = out.shape[0] // 2
    high, low = split(decode(codes, scale))
    out[pl.ds(0, rows), :] = high
    out[pl.ds(rows, rows), :] = low


def near_columns_kernel(code0, code1, code2, out_ref):
    rows = out_ref.shape[1] // 2
    for d, ref in enumerate((code0, code1, code2)):

        @pl.when(pl.program_id(0) == d)
        def _():
            value_pair(ref[pl.ds(0, rows), :], lane_scale(ref[pl.ds(rows, 16), :], 1.0), out_ref.at[0])


def far_columns_kernel(at_ref, rows_ref, code1, code2, upper, lower, out_ref, design_ref):
    q = at_ref[0]
    rows = out_ref.shape[1] // 2
    half, share, n_pts = upper.shape[0], rows_ref.shape[0], rows_ref.shape[1]
    scale = lane_scale(lower[pl.ds(rows - half, 16), :], 1.0)
    codes = jnp.concatenate([upper[...], lower[pl.ds(0, rows - half), :]], axis=0)
    value_pair(codes, scale, out_ref.at[0])
    start = pl.multiple_of(q * share, share)

    def put(d, value):
        at = pl.multiple_of(jnp.bitwise_xor(q, d) * n_pts, n_pts)
        design_ref[:, pl.ds(at, n_pts)] = value

    put(0, rows_ref[...])
    for d, ref in ((1, code1), (2, code2)):
        put(d, decode(ref[pl.ds(start, share), :], lane_scale(ref[pl.ds(rows, 16), :], 1.0)))

    @pl.when(start < half)
    def _():
        put(3, decode(upper[pl.ds(start, share), :], scale))

    @pl.when(start >= half)
    def _():
        put(3, decode(lower[pl.ds(pl.multiple_of(start - half, share), share), :], scale))


def gray(value):
    return jnp.bitwise_xor(value, lax.shift_right_logical(value, 1))


def ring_source(z, steps):
    return gray(jnp.bitwise_and(gray(z) - steps, 3))


def gram_kernel(steps, first, n_near, at_ref, *refs):
    n_codes = 2 * len(steps)
    codes, value_refs, out_ref, left = refs[:n_codes], refs[n_codes:-2], refs[-2], refs[-1]
    n, j = pl.program_id(0), pl.program_id(1)
    k, z, core = at_ref[0], at_ref[1], at_ref[2]
    source = ring_source(z, steps[0] + n)
    n_pts = out_ref.shape[1]
    rows = codes[0].shape[1]
    for i in range(len(steps)):

        @pl.when((j == 0) & (n == i))
        def _():
            for ref, side in ((codes[2 * i], core), (codes[2 * i + 1], 1 - core)):
                scale = lane_scale(ref[pl.ds(n_pts, 16), :], 1.0 / rows)
                high, low = split(decode(ref[pl.ds(0, n_pts), :], scale))
                left[side, :, pl.ds(0, rows)] = high
                left[side, :, pl.ds(rows, rows)] = low

    def multiply(pair_ref):
        for side in range(2):
            high, low = left[side, :, pl.ds(0, rows)], left[side, :, pl.ds(rows, rows)]
            top, rest = pair_ref[0, pl.ds(0, rows), :], pair_ref[0, pl.ds(rows, rows), :]
            out_ref[side] = dot_nn(high, top) + dot_nn(low, top) + dot_nn(high, rest)

    if first == 0 and n_near < 4:
        multiply(value_refs[0])
    elif first == 3:
        multiply(value_refs[0])
    else:
        pl.when(j < 3)(lambda: multiply(value_refs[0]))
        pl.when(j == 3)(lambda: multiply(value_refs[1]))

    @pl.when((k == z) & (jnp.bitwise_xor(k, first + j) == source))
    def _():
        eye = lax.broadcasted_iota(jnp.int32, out_ref.shape[1:], 0) == lax.broadcasted_iota(
            jnp.int32, out_ref.shape[1:], 1
        )
        out_ref[core] = out_ref[core] + jnp.where(eye, damping, 0.0)


def cost(multiply_adds, nbytes):
    return pl.CostEstimate(flops=2 * multiply_adds, bytes_accessed=nbytes, transcendentals=0)


def whole(shape):
    return pl.BlockSpec(shape, lambda *_: (0,) * len(shape))


def on_device(env_desc, point_desc, pool_index, pool_count, pool_weight, row_dest):
    groups, planes = 4, 4
    q = lax.axis_index("rows")
    p = lax.axis_index("pts")
    z, core = p // 2, p % 2
    at = jnp.stack([q, z, core]).astype(jnp.int32)
    n_rows = pool_index.shape[0] * groups // 2
    envs, part = env_desc.shape
    n_pts = point_desc.shape[0] // planes
    comps = point_desc.shape[1]
    n_pool = pool_index.shape[1]
    pad = n_rows + 16

    def permutation(to):
        return [
            (r * 8 + s, to(r, s // 2, s % 2)[0] * 8 + to(r, s // 2, s % 2)[1] * 2 + to(r, s // 2, s % 2)[2])
            for r in range(groups)
            for s in range(planes * 2)
        ]

    def moved(value, to):
        return lax.ppermute(value, BOTH, permutation(to))

    along_x = lambda r, h, c: (r ^ 1, h, c)
    along_y = lambda r, h, c: (r ^ 2, h, c)
    to_core = lambda r, h, c: (r, h, 1 - c)
    ring = (1, 3, 0, 2)
    along_z = lambda r, h, c: (r, ring[h], c)


    members = jnp.arange(n_pool, dtype=jnp.int32)
    live = jnp.where(members[None, :] < pool_count[:, None], pool_weight, 0.0).T
    live_high = lax.reduce_precision(live, 8, 7)
    rest = live - live_high
    rest_high = lax.reduce_precision(rest, 8, 7)
    place = row_dest[None, :] + 1
    index = pool_index.T
    table = jnp.concatenate(
        [
            (index // 256).astype(BF16),
            (index % 256).astype(BF16),
            live_high.astype(BF16),
            rest_high.astype(BF16),
            (rest - rest_high).astype(BF16),
            (place // 256).astype(BF16),
            (place % 256).astype(BF16),
            jnp.zeros((10, index.shape[1]), BF16),
        ],
        axis=0,
    )
    quarters = point_desc.reshape(planes, n_pts, comps)
    table = jnp.broadcast_to(table[None], (groups, *table.shape))
    outbox = jnp.concatenate([quarters, table], axis=1)

    cols_pts = lax.all_to_all(outbox, "rows", 0, 0, tiled=True)
    own = jnp.stack(
        [env_desc, *(moved(env_desc, lambda r, h, c, d=d: (r, h ^ d, c)) for d in (1, 2, 3))]
    )
    own, quarters = lax.optimization_barrier((own, quarters))
    env_mine = lax.all_to_all(
        jnp.broadcast_to(own[None], (groups, *own.shape)), "rows", 0, 0, tiled=True
    )

    panel_pts = [
        moved(
            lax.dynamic_index_in_dim(quarters, q ^ t, 0, keepdims=False),
            lambda r, h, c, t=t: (h, r ^ t, c),
        )
        for t in range(planes)
    ]

    table_rows = table.shape[1]
    high, low = pl.pallas_call(
        weights_kernel,
        grid=(1,),
        in_specs=[pl.BlockSpec((groups, table_rows, comps), lambda _: (0, n_pts // table_rows, 0))],
        out_specs=[whole((groups, n_rows, envs))] * 2,
        out_shape=[jax.ShapeDtypeStruct((groups, n_rows, envs), BF16)] * 2,
        compiler_params=pltpu.CompilerParams(vmem_limit_bytes=VMEM_LIMIT),
        cost_estimate=cost(n_rows * n_rows * groups * 16 * 6, 4 * MIB),
        name="pool_weights",
    )(cols_pts)

    env_mine, high, low, *panel_pts = lax.optimization_barrier((env_mine, high, low, *panel_pts))
    env_swapped = moved(env_mine, to_core)

    anywhere = pl.BlockSpec(memory_space=pl.ANY)

    pts_scratch = pltpu.VMEM((n_pts, groups * comps), BF16)
    cols_code, panel_code, own_rows = pl.pallas_call(
        design_kernel,
        grid_spec=pltpu.PrefetchScalarGridSpec(
            num_scalar_prefetch=1,
            grid=(1,),
            in_specs=[anywhere] * 9,
            out_specs=[
                whole((pad, n_pts)),
                whole((n_pts + 16, n_rows)),
                whole((n_rows // groups, n_pts)),
            ],
            scratch_shapes=[
                pts_scratch,
                pts_scratch,
                pltpu.VMEM((groups, envs, groups * comps), BF16),
                pltpu.VMEM((groups, 2, n_rows, envs), BF16),
                pltpu.VMEM((n_rows, n_pts), F32),
                pltpu.VMEM((n_pts, n_rows), F32),
                pltpu.SemaphoreType.DMA((8,)),
                pltpu.SemaphoreType.DMA((4, 10)),
            ],
        ),
        out_shape=[
            jax.ShapeDtypeStruct((pad, n_pts), jnp.int16),
            jax.ShapeDtypeStruct((n_pts + 16, n_rows), jnp.int16),
            jax.ShapeDtypeStruct((n_rows // groups, n_pts), F32),
        ],
        compiler_params=pltpu.CompilerParams(vmem_limit_bytes=VMEM_LIMIT),
        cost_estimate=cost(8 * n_pts * envs * (groups * comps + 3 * n_rows), 14 * MIB),
        name="design_values",
    )(at, env_mine, env_swapped, cols_pts, *panel_pts, high, low)

    half = n_rows // 2
    held = [panel_code, moved(panel_code, along_z)]
    from_x, from_y = moved(cols_code, along_x), moved(cols_code, along_y)
    swapped = [moved(panel_code, to_core)]
    upper, lower = moved(from_x[:half], along_y), moved(from_y[half:], along_x)
    width = groups * n_pts
    code_spec = whole((pad, n_pts))
    near = pl.pallas_call(
        near_columns_kernel,
        grid=(3,),
        in_specs=[code_spec] * 3,
        out_specs=pl.BlockSpec((1, 2 * n_rows, n_pts), lambda d: (d, 0, 0)),
        out_shape=jax.ShapeDtypeStruct((3, 2 * n_rows, n_pts), BF16),
        compiler_params=pltpu.CompilerParams(vmem_limit_bytes=VMEM_LIMIT),
        cost_estimate=cost(0, 6 * MIB),
        name="near_columns",
    )(cols_code, from_x, from_y)
    far, design = pl.pallas_call(
        far_columns_kernel,
        grid_spec=pltpu.PrefetchScalarGridSpec(
            num_scalar_prefetch=1,
            grid=(1,),
            in_specs=[
                whole((n_rows // groups, n_pts)),
                code_spec,
                code_spec,
                whole((half, n_pts)),
                whole((pad - half, n_pts)),
            ],
            out_specs=[whole((1, 2 * n_rows, n_pts)), whole((n_rows // groups, width))],
        ),
        out_shape=[
            jax.ShapeDtypeStruct((1, 2 * n_rows, n_pts), BF16),
            jax.ShapeDtypeStruct((n_rows // groups, width), F32),
        ],
        compiler_params=pltpu.CompilerParams(vmem_limit_bytes=VMEM_LIMIT),
        cost_estimate=cost(0, 5 * MIB),
        name="far_columns",
    )(at, own_rows, from_x, from_y, upper, lower)

    panel_spec = whole((n_pts + 16, n_rows))

    def gram_rows(gram, steps, first, n_near):
        values, value_specs = [], []
        if first < 3:
            values.append(near)
            value_specs.append(
                pl.BlockSpec((1, 2 * n_rows, n_pts), lambda n, j, _: (jnp.minimum(j, 2), 0, 0))
            )
        if first + n_near == 4:
            values.append(far)
            value_specs.append(whole((1, 2 * n_rows, n_pts)))
        operands = [at, *(c for i in steps for c in (held[i], swapped[i])), *values]
        in_specs = [panel_spec] * (2 * len(steps)) + value_specs
        aliases = {}
        if gram is not None:
            aliases = {len(operands): 0}
            in_specs.append(anywhere)
            operands.append(gram)
        return pl.pallas_call(
            functools.partial(gram_kernel, steps, first, n_near),
            grid_spec=pltpu.PrefetchScalarGridSpec(
                num_scalar_prefetch=1,
                grid=(len(steps), n_near),
                in_specs=in_specs,
                out_specs=pl.BlockSpec(
                    (2, n_pts, n_pts),
                    lambda n, j, s: (0, ring_source(s[1], steps[0] + n), jnp.bitwise_xor(s[0], first + j)),
                ),
                scratch_shapes=[pltpu.VMEM((2, n_pts, 2 * n_rows), BF16)],
            ),
            out_shape=jax.ShapeDtypeStruct((2, planes * n_pts, width), F32),
            input_output_aliases=aliases,
            compiler_params=pltpu.CompilerParams(vmem_limit_bytes=VMEM_LIMIT),
            cost_estimate=cost(len(steps) * n_near * 8 * n_pts * n_pts * n_rows, 4 * MIB),
            name="gram_rows",
        )(*operands)

    held.append(moved(held[1], along_z))
    swapped.append(moved(held[1], to_core))
    gram = gram_rows(None, (0,), 0, 3)
    gram = gram_rows(gram, (1,), 0, 3)
    held[2], gram = lax.optimization_barrier((held[2], gram))
    held.append(moved(held[2], along_z))
    swapped.append(moved(held[2], to_core))
    gram = gram_rows(gram, (0, 1), 3, 1)
    held[3], gram = lax.optimization_barrier((held[3], gram))
    swapped.append(moved(held[3], to_core))
    gram = gram_rows(gram, (2,), 0, 4)
    gram = gram_rows(gram, (3,), 0, 4)
    return design, gram.reshape(2 * planes * n_pts, width)


def solution(mesh):
    in_specs = (
        P("rows", "pts"),
        P("pts", "rows"),
        P("rows", None),
        P("rows"),
        P("rows", None),
        P("rows"),
    )
    out_specs = (P("rows", "pts"), P("rows", "pts"))
    body = on_device if dict(mesh.shape) == {"rows": 4, "pts": 8} else on_any_device
    return jax.shard_map(body, mesh=mesh, in_specs=in_specs, out_specs=out_specs, check_vma=False)
```

```python
import functools

import jax
import jax.numpy as jnp
from jax import lax
from jax.experimental import pallas as pl
from jax.experimental.pallas import tpu as pltpu
from jax.sharding import PartitionSpec as P

damping = 0.5
CODE_TOP = 32700.0
BOTH = ("rows", "pts")
MIB = 1 << 20
VMEM_LIMIT = 63 * MIB
F32 = jnp.float32
BF16 = jnp.bfloat16


def from_root(value, axis, source):
    kept = jnp.where(lax.axis_index(axis) == source, value, 0).astype(value.dtype)
    return lax.psum(kept, axis)


def kernel_values(left, right):
    products = lax.dot_general(
        left, right, (((1,), (1,)), ((), ())), preferred_element_type=jnp.float32
    )
    scaled = products * left.shape[1] ** (-0.5)
    squared = scaled * scaled
    return 0.25 * squared * squared


def live_weights(pool_count, pool_weight):
    members = jnp.arange(pool_weight.shape[1], dtype=jnp.int32)
    return jnp.where(members[None, :] < pool_count[:, None], pool_weight, 0.0)


def pool_rows(kernel_table, env_index, weights_live):
    pooled = jnp.zeros((env_index.shape[0], kernel_table.shape[1]), jnp.float32)
    for member in range(env_index.shape[1]):
        pooled = pooled + weights_live[:, member : member + 1] * kernel_table[env_index[:, member]]
    return pooled


def on_any_device(env_desc, point_desc, pool_index, pool_count, pool_weight, row_dest):
    groups = lax.axis_size("rows")
    slot_total = pool_index.shape[0]
    balanced = slot_total // 2
    slot_share = slot_total // groups
    points = lax.all_gather(point_desc, "rows", axis=1, tiled=True)
    width_pts = points.shape[0]
    weights_live = live_weights(pool_count, pool_weight)
    live_slot = row_dest >= 0
    owner_group = jnp.where(live_slot, row_dest // balanced, groups)
    within = jnp.where(live_slot, row_dest % balanced, balanced)
    owner_table = (owner_group[:, None] == jnp.arange(groups, dtype=jnp.int32)[None, :]).astype(
        jnp.int32
    )
    earlier = jnp.cumsum(owner_table, axis=0) - owner_table
    slot_rank = jnp.sum(earlier * owner_table, axis=1)
    outbox_place = (
        jnp.full((groups, slot_share), balanced, jnp.int32)
        .at[owner_group, slot_rank]
        .set(within, mode="drop")
    )
    features = lax.all_gather(env_desc, "pts", axis=1, tiled=True)
    slot_rows = pool_rows(kernel_values(features, points), pool_index, weights_live)
    outbox = (
        jnp.zeros((groups, slot_share, width_pts), jnp.float32)
        .at[owner_group, slot_rank]
        .set(slot_rows, mode="drop")
    )
    inbox_rows, inbox_place = (
        lax.all_to_all(outbox, "rows", split_axis=0, concat_axis=0, tiled=True),
        lax.all_to_all(outbox_place, "rows", split_axis=0, concat_axis=0, tiled=True),
    )
    design = (
        jnp.zeros((balanced, width_pts), jnp.float32)
        .at[inbox_place.reshape(-1)]
        .set(inbox_rows.reshape(-1, width_pts), mode="drop")
    )
    all_rows = lax.all_gather(design, "rows", axis=0, tiled=True)
    per_group = lax.axis_size("pts") // groups
    row_group = lax.axis_index("rows")
    pieces = []
    for part_index in range(per_group):
        diagonal_panel = from_root(all_rows, "pts", row_group * per_group + part_index)
        pieces.append(
            lax.dot_general(
                diagonal_panel,
                all_rows,
                (((0,), (0,)), ((), ())),
                precision=lax.Precision.HIGHEST,
                preferred_element_type=jnp.float32,
            )
        )
    gram_tile = jnp.concatenate(pieces, axis=0) * (1.0 / all_rows.shape[0])
    tile_rows = gram_tile.shape[0]
    row_ids = row_group * tile_rows + jnp.arange(tile_rows, dtype=jnp.int32)
    col_ids = lax.axis_index("pts") * width_pts + jnp.arange(width_pts, dtype=jnp.int32)
    gram_tile = gram_tile + jnp.where(row_ids[:, None] == col_ids[None, :], damping, 0.0)
    return (design, gram_tile)


def dot_nn(a, b):
    return lax.dot_general(a, b, (((1,), (0,)), ((), ())), preferred_element_type=F32)


def dot_nt(a, b):
    return lax.dot_general(a, b, (((1,), (1,)), ((), ())), preferred_element_type=F32)


def split(value):
    high = value.astype(BF16)
    return high, (value - high.astype(F32)).astype(BF16)


def encode(value, code_ref):
    n = value.shape[0]
    size = jnp.abs(value)
    top = jnp.maximum(jnp.max(size, axis=0, keepdims=True), 1e-30)
    exponent = jnp.ceil(jnp.log(top) * 1.4426950408889634)
    root = jnp.sqrt(size * jnp.exp2(-exponent))
    code = jnp.minimum(root * CODE_TOP + 0.5, 32767.0).astype(jnp.int32)
    code_ref[pl.ds(0, n), :] = jnp.where(value < 0, -code, code).astype(jnp.int16)
    pad = code_ref.shape[0] - n
    code_ref[pl.ds(n, pad), :] = jnp.broadcast_to(
        exponent.astype(jnp.int32), (pad, value.shape[1])
    ).astype(jnp.int16)


def lane_scale(exponent_rows, extra):
    exponent = exponent_rows.astype(jnp.int32).astype(F32)[0:1, :]
    return jnp.exp2(exponent) * (extra / (CODE_TOP * CODE_TOP))


def decode(codes, scale):
    root = codes.astype(jnp.int32).astype(F32)
    return root * jnp.abs(root) * scale


def weights_kernel(*refs):
    tables, high_ref, low_ref = refs[:-2], refs[-2], refs[-1]
    rows, envs = high_ref.shape[1:]
    for d, ref in enumerate(tables):
        lanes = ref.shape[1]
        piece = ref[...].astype(F32)
        piece = jnp.concatenate([piece[0:32], piece[32:64]], axis=1)
        slots = 2 * lanes
        index = piece[0:4] * 256.0 + piece[4:8]
        weight = piece[8:12] + piece[12:16] + piece[16:20]
        place = piece[20:21] * 256.0 + piece[21:22] - 1.0
        row_id = lax.broadcasted_iota(jnp.int32, (rows, slots), 0).astype(F32)
        by_row = lax.dot_general(
            jnp.where(place == row_id, 1.0, 0.0),
            jnp.concatenate([index, weight], axis=0),
            (((1,), (1,)), ((), ())),
            precision=lax.Precision.HIGHEST,
            preferred_element_type=F32,
        )
        env_id = lax.broadcasted_iota(jnp.int32, (rows, envs), 1).astype(F32)
        index = jnp.floor(by_row + 0.5)
        total = jnp.zeros((rows, envs), F32)
        for member in range(4):
            total = total + jnp.where(
                index[:, member : member + 1] == env_id, by_row[:, 4 + member : 5 + member], 0.0
            )
        high, low = split(total)
        high_ref[d] = high
        low_ref[d] = low


def fourth_power(products, scale):
    s = products * scale
    s = s * s
    return split(0.25 * s * s)


def add_columns(features, weights, pts, total, first):
    high, low = weights[0], weights[1]
    k_high, k_low = fourth_power(dot_nt(features, pts[...]), features.shape[1] ** (-0.5))
    part = dot_nn(high, k_high) + dot_nn(high, k_low) + dot_nn(low, k_high)
    total[...] = part if first else total[...] + part


def add_panel(features, weights, pts, total, first):
    high, low = weights[0], weights[1]
    k_high, k_low = fourth_power(dot_nt(pts[...], features), features.shape[1] ** (-0.5))
    part = dot_nt(k_high, high) + dot_nt(k_low, high) + dot_nt(k_high, low)
    total[...] = part if first else total[...] + part


def started(copies):
    for copy in copies:
        copy.start()
    return copies


def waited(copies):
    for copy in copies:
        copy.wait()


def group_copies(at_ref, d, sides, weights_from, env, weights, sems):
    z, core = at_ref[1], at_ref[2]
    envs, part = env.shape[0], sides[0][0].shape[1]
    out = []
    for side, refs in zip((core, 1 - core), sides):
        for r in range(4):
            ref, first = (refs[d], r) if d < 3 else (refs[3 + r // 2], r % 2)
            at = pl.multiple_of((jnp.bitwise_xor(z, r) * 2 + side) * part, part)
            source = ref.at[pl.ds(first * envs, envs)]
            out.append(pltpu.make_async_copy(source, env.at[:, pl.ds(at, part)], sems.at[len(out)]))
    for i in range(2):
        source = weights_from[i].at[d] if d < 3 else weights_from[2 + i].at[0]
        out.append(pltpu.make_async_copy(source, weights.at[i], sems.at[8 + i]))
    return out


def design_kernel(at_ref, *refs):
    sides, cols, panels, weights_from = (refs[0:5], refs[5:10]), refs[10], refs[11:15], refs[15:19]
    cols_code, panel_code, rows_out = refs[19:22]
    cols_pts, panel_pts, env, weights, cols_sum, panel_sum, point_sems, group_sems = refs[22:]
    q, z = at_ref[0], at_ref[1]
    n_pts, comps = panels[0].shape
    points = []
    for j in range(4):
        to = cols_pts.at[:, pl.ds(j * comps, comps)]
        points.append(pltpu.make_async_copy(cols.at[j], to, point_sems.at[j]))
    started(points)
    copies = [
        group_copies(at_ref, d, sides, weights_from, env.at[d], weights.at[d], group_sems.at[d])
        for d in range(4)
    ]
    started(copies[0])
    panel = []
    for t, ref in enumerate(panels):
        at = pl.multiple_of(jnp.bitwise_xor(z, t) * comps, comps)
        to = panel_pts.at[:, pl.ds(at, comps)]
        panel.append(pltpu.make_async_copy(ref, to, point_sems.at[4 + t]))
    started(panel)
    for d in range(1, 4):
        started(copies[d])
    waited(points)
    for d in range(4):
        waited(copies[d])
        add_columns(env[d], weights.at[d], cols_pts, cols_sum, d == 0)
        if d == 0:
            waited(panel)
        add_panel(env[d], weights.at[d], panel_pts, panel_sum, d == 0)
    encode(cols_sum[...], cols_code)
    share = rows_out.shape[0]
    rows_out[...] = cols_sum[pl.ds(pl.multiple_of(q * share, share), share), :]
    encode(panel_sum[...], panel_code)


def value_pair(codes, scale, out):
    rows = out.shape[0] // 2
    high, low = split(decode(codes, scale))
    out[pl.ds(0, rows), :] = high
    out[pl.ds(rows, rows), :] = low


def near_columns_kernel(code0, code1, code2, out_ref):
    rows = out_ref.shape[1] // 2
    for d, ref in enumerate((code0, code1, code2)):

        @pl.when(pl.program_id(0) == d)
        def _():
            value_pair(ref[pl.ds(0, rows), :], lane_scale(ref[pl.ds(rows, 16), :], 1.0), out_ref.at[0])


def far_columns_kernel(at_ref, rows_ref, code1, code2, upper, lower, out_ref, design_ref):
    q = at_ref[0]
    rows = out_ref.shape[1] // 2
    half, share, n_pts = upper.shape[0], rows_ref.shape[0], rows_ref.shape[1]
    scale = lane_scale(lower[pl.ds(rows - half, 16), :], 1.0)
    codes = jnp.concatenate([upper[...], lower[pl.ds(0, rows - half), :]], axis=0)
    value_pair(codes, scale, out_ref.at[0])
    start = pl.multiple_of(q * share, share)

    def put(d, value):
        at = pl.multiple_of(jnp.bitwise_xor(q, d) * n_pts, n_pts)
        design_ref[:, pl.ds(at, n_pts)] = value

    put(0, rows_ref[...])
    for d, ref in ((1, code1), (2, code2)):
        put(d, decode(ref[pl.ds(start, share), :], lane_scale(ref[pl.ds(rows, 16), :], 1.0)))

    @pl.when(start < half)
    def _():
        put(3, decode(upper[pl.ds(start, share), :], scale))

    @pl.when(start >= half)
    def _():
        put(3, decode(lower[pl.ds(pl.multiple_of(start - half, share), share), :], scale))


def gray(value):
    return jnp.bitwise_xor(value, lax.shift_right_logical(value, 1))


def ring_source(z, steps):
    return gray(jnp.bitwise_and(gray(z) - steps, 3))


def gram_kernel(steps, first, n_near, at_ref, *refs):
    n_codes = 2 * len(steps)
    codes, value_refs, out_ref, left = refs[:n_codes], refs[n_codes:-2], refs[-2], refs[-1]
    n, j = pl.program_id(0), pl.program_id(1)
    k, z, core = at_ref[0], at_ref[1], at_ref[2]
    source = ring_source(z, steps[0] + n)
    n_pts = out_ref.shape[1]
    rows = codes[0].shape[1]
    for i in range(len(steps)):

        @pl.when((j == 0) & (n == i))
        def _():
            for ref, side in ((codes[2 * i], core), (codes[2 * i + 1], 1 - core)):
                scale = lane_scale(ref[pl.ds(n_pts, 16), :], 1.0 / rows)
                high, low = split(decode(ref[pl.ds(0, n_pts), :], scale))
                left[side, :, pl.ds(0, rows)] = high
                left[side, :, pl.ds(rows, rows)] = low

    def multiply(pair_ref):
        for side in range(2):
            high, low = left[side, :, pl.ds(0, rows)], left[side, :, pl.ds(rows, rows)]
            top, rest = pair_ref[0, pl.ds(0, rows), :], pair_ref[0, pl.ds(rows, rows), :]
            out_ref[side] = dot_nn(high, top) + dot_nn(low, top) + dot_nn(high, rest)

    if first == 0 and n_near < 4:
        multiply(value_refs[0])
    elif first == 3:
        multiply(value_refs[0])
    else:
        pl.when(j < 3)(lambda: multiply(value_refs[0]))
        pl.when(j == 3)(lambda: multiply(value_refs[1]))

    @pl.when((k == z) & (jnp.bitwise_xor(k, first + j) == source))
    def _():
        eye = lax.broadcasted_iota(jnp.int32, out_ref.shape[1:], 0) == lax.broadcasted_iota(
            jnp.int32, out_ref.shape[1:], 1
        )
        out_ref[core] = out_ref[core] + jnp.where(eye, damping, 0.0)


def cost(multiply_adds, nbytes):
    return pl.CostEstimate(flops=2 * multiply_adds, bytes_accessed=nbytes, transcendentals=0)


def whole(shape):
    return pl.BlockSpec(shape, lambda *_: (0,) * len(shape))


def on_device(env_desc, point_desc, pool_index, pool_count, pool_weight, row_dest):
    groups, planes = 4, 4
    q = lax.axis_index("rows")
    p = lax.axis_index("pts")
    z, core = p // 2, p % 2
    at = jnp.stack([q, z, core]).astype(jnp.int32)
    n_rows = pool_index.shape[0] * groups // 2
    envs, part = env_desc.shape
    n_pts = point_desc.shape[0] // planes
    comps = point_desc.shape[1]
    n_pool = pool_index.shape[1]
    pad = n_rows + 16

    def permutation(to):
        return [
            (r * 8 + s, to(r, s // 2, s % 2)[0] * 8 + to(r, s // 2, s % 2)[1] * 2 + to(r, s // 2, s % 2)[2])
            for r in range(groups)
            for s in range(planes * 2)
        ]

    def moved(value, to):
        return lax.ppermute(value, BOTH, permutation(to))

    along_x = lambda r, h, c: (r ^ 1, h, c)
    along_y = lambda r, h, c: (r ^ 2, h, c)
    to_core = lambda r, h, c: (r, h, 1 - c)
    ring = (1, 3, 0, 2)
    along_z = lambda r, h, c: (r, ring[h], c)


    quarters = point_desc.reshape(planes, n_pts, comps)
    cols_pts = lax.all_to_all(quarters, "rows", 0, 0, tiled=True)

    members = jnp.arange(n_pool, dtype=jnp.int32)
    live = jnp.where(members[None, :] < pool_count[:, None], pool_weight, 0.0).T
    live_high = lax.reduce_precision(live, 8, 7)
    rest = live - live_high
    rest_high = lax.reduce_precision(rest, 8, 7)
    place = row_dest[None, :] + 1
    index = pool_index.T
    table = jnp.concatenate(
        [
            (index // 256).astype(BF16),
            (index % 256).astype(BF16),
            live_high.astype(BF16),
            rest_high.astype(BF16),
            (rest - rest_high).astype(BF16),
            (place // 256).astype(BF16),
            (place % 256).astype(BF16),
            jnp.zeros((10, index.shape[1]), BF16),
        ],
        axis=0,
    )

    own = jnp.concatenate(
        [
            env_desc,
            *(moved(env_desc, lambda r, h, c, d=d: (r, h ^ d, c)) for d in (1, 2, 3)),
            table[:, :part],
            table[:, part:],
        ]
    )
    own, cols_pts, quarters = lax.optimization_barrier((own, cols_pts, quarters))
    near_x, near_y = moved(own, along_x), moved(own, along_y)
    swap_own = moved(own, to_core)

    panel_pts = [
        moved(
            lax.dynamic_index_in_dim(quarters, q ^ t, 0, keepdims=False),
            lambda r, h, c, t=t: (h, r ^ t, c),
        )
        for t in range(planes)
    ]

    def pool_weights(tables):
        n = len(tables)
        return pl.pallas_call(
            weights_kernel,
            grid=(1,),
            in_specs=[
                pl.BlockSpec((64, part), lambda _, last=t.shape[0] // 64 - 1: (last, 0))
                for t in tables
            ],
            out_specs=[whole((n, n_rows, envs))] * 2,
            out_shape=[jax.ShapeDtypeStruct((n, n_rows, envs), BF16)] * 2,
            compiler_params=pltpu.CompilerParams(vmem_limit_bytes=VMEM_LIMIT),
            cost_estimate=cost(n * n_rows * n_rows * 16 * 6, n * MIB),
            name="pool_weights",
        )(*tables)

    far_upper, far_lower = moved(near_x[: 2 * envs], along_y), moved(near_y[2 * envs :], along_x)
    near_weights = pool_weights([own, near_x, near_y])
    far_upper, far_lower, *rest = lax.optimization_barrier(
        (far_upper, far_lower, *near_weights, *panel_pts)
    )
    near_weights, panel_pts = rest[:2], rest[2:]
    mine = (own, near_x, near_y, far_upper, far_lower)
    other = (swap_own, *(moved(e, to_core) for e in mine[1:]))
    weights = (*near_weights, *pool_weights([far_lower]))

    anywhere = pl.BlockSpec(memory_space=pl.ANY)

    pts_scratch = pltpu.VMEM((n_pts, groups * comps), BF16)
    cols_code, panel_code, own_rows = pl.pallas_call(
        design_kernel,
        grid_spec=pltpu.PrefetchScalarGridSpec(
            num_scalar_prefetch=1,
            grid=(1,),
            in_specs=[anywhere] * 19,
            out_specs=[
                whole((pad, n_pts)),
                whole((n_pts + 16, n_rows)),
                whole((n_rows // groups, n_pts)),
            ],
            scratch_shapes=[
                pts_scratch,
                pts_scratch,
                pltpu.VMEM((groups, envs, groups * comps), BF16),
                pltpu.VMEM((groups, 2, n_rows, envs), BF16),
                pltpu.VMEM((n_rows, n_pts), F32),
                pltpu.VMEM((n_pts, n_rows), F32),
                pltpu.SemaphoreType.DMA((8,)),
                pltpu.SemaphoreType.DMA((4, 10)),
            ],
        ),
        out_shape=[
            jax.ShapeDtypeStruct((pad, n_pts), jnp.int16),
            jax.ShapeDtypeStruct((n_pts + 16, n_rows), jnp.int16),
            jax.ShapeDtypeStruct((n_rows // groups, n_pts), F32),
        ],
        compiler_params=pltpu.CompilerParams(vmem_limit_bytes=VMEM_LIMIT),
        cost_estimate=cost(8 * n_pts * envs * (groups * comps + 3 * n_rows), 14 * MIB),
        name="design_values",
    )(at, *mine, *other, cols_pts, *panel_pts, *weights)

    half = n_rows // 2
    held = [panel_code, moved(panel_code, along_z)]
    from_x, from_y = moved(cols_code, along_x), moved(cols_code, along_y)
    swapped = [moved(panel_code, to_core)]
    upper, lower = moved(from_x[:half], along_y), moved(from_y[half:], along_x)
    width = groups * n_pts
    code_spec = whole((pad, n_pts))
    near = pl.pallas_call(
        near_columns_kernel,
        grid=(3,),
        in_specs=[code_spec] * 3,
        out_specs=pl.BlockSpec((1, 2 * n_rows, n_pts), lambda d: (d, 0, 0)),
        out_shape=jax.ShapeDtypeStruct((3, 2 * n_rows, n_pts), BF16),
        compiler_params=pltpu.CompilerParams(vmem_limit_bytes=VMEM_LIMIT),
        cost_estimate=cost(0, 6 * MIB),
        name="near_columns",
    )(cols_code, from_x, from_y)
    far, design = pl.pallas_call(
        far_columns_kernel,
        grid_spec=pltpu.PrefetchScalarGridSpec(
            num_scalar_prefetch=1,
            grid=(1,),
            in_specs=[
                whole((n_rows // groups, n_pts)),
                code_spec,
                code_spec,
                whole((half, n_pts)),
                whole((pad - half, n_pts)),
            ],
            out_specs=[whole((1, 2 * n_rows, n_pts)), whole((n_rows // groups, width))],
        ),
        out_shape=[
            jax.ShapeDtypeStruct((1, 2 * n_rows, n_pts), BF16),
            jax.ShapeDtypeStruct((n_rows // groups, width), F32),
        ],
        compiler_params=pltpu.CompilerParams(vmem_limit_bytes=VMEM_LIMIT),
        cost_estimate=cost(0, 5 * MIB),
        name="far_columns",
    )(at, own_rows, from_x, from_y, upper, lower)

    panel_spec = whole((n_pts + 16, n_rows))

    def gram_rows(gram, steps, first, n_near):
        values, value_specs = [], []
        if first < 3:
            values.append(near)
            value_specs.append(
                pl.BlockSpec((1, 2 * n_rows, n_pts), lambda n, j, _: (jnp.minimum(j, 2), 0, 0))
            )
        if first + n_near == 4:
            values.append(far)
            value_specs.append(whole((1, 2 * n_rows, n_pts)))
        operands = [at, *(c for i in steps for c in (held[i], swapped[i])), *values]
        in_specs = [panel_spec] * (2 * len(steps)) + value_specs
        aliases = {}
        if gram is not None:
            aliases = {len(operands): 0}
            in_specs.append(anywhere)
            operands.append(gram)
        return pl.pallas_call(
            functools.partial(gram_kernel, steps, first, n_near),
            grid_spec=pltpu.PrefetchScalarGridSpec(
                num_scalar_prefetch=1,
                grid=(len(steps), n_near),
                in_specs=in_specs,
                out_specs=pl.BlockSpec(
                    (2, n_pts, n_pts),
                    lambda n, j, s: (0, ring_source(s[1], steps[0] + n), jnp.bitwise_xor(s[0], first + j)),
                ),
                scratch_shapes=[pltpu.VMEM((2, n_pts, 2 * n_rows), BF16)],
            ),
            out_shape=jax.ShapeDtypeStruct((2, planes * n_pts, width), F32),
            input_output_aliases=aliases,
            compiler_params=pltpu.CompilerParams(vmem_limit_bytes=VMEM_LIMIT),
            cost_estimate=cost(len(steps) * n_near * 8 * n_pts * n_pts * n_rows, 4 * MIB),
            name="gram_rows",
        )(*operands)

    held.append(moved(held[1], along_z))
    swapped.append(moved(held[1], to_core))
    gram = gram_rows(None, (0, 1), 0, 3)
    held[2], gram = lax.optimization_barrier((held[2], gram))
    held.append(moved(held[2], along_z))
    swapped.append(moved(held[2], to_core))
    gram = gram_rows(gram, (0, 1), 3, 1)
    held[3], gram = lax.optimization_barrier((held[3], gram))
    swapped.append(moved(held[3], to_core))
    gram = gram_rows(gram, (2,), 0, 4)
    gram = gram_rows(gram, (3,), 0, 4)
    return design, gram.reshape(2 * planes * n_pts, width)


def solution(mesh):
    in_specs = (
        P("rows", "pts"),
        P("pts", "rows"),
        P("rows", None),
        P("rows"),
        P("rows", None),
        P("rows"),
    )
    out_specs = (P("rows", "pts"), P("rows", "pts"))
    body = on_device if dict(mesh.shape) == {"rows": 4, "pts": 8} else on_any_device
    return jax.shard_map(body, mesh=mesh, in_specs=in_specs, out_specs=out_specs, check_vma=False)
```

```python
import functools

import jax
import jax.numpy as jnp
from jax import lax
from jax.experimental import pallas as pl
from jax.experimental.pallas import tpu as pltpu
from jax.sharding import PartitionSpec as P

damping = 0.5
CODE_TOP = 32700.0
BOTH = ("rows", "pts")
MIB = 1 << 20
VMEM_LIMIT = 63 * MIB
F32 = jnp.float32
BF16 = jnp.bfloat16


def from_root(value, axis, source):
    kept = jnp.where(lax.axis_index(axis) == source, value, 0).astype(value.dtype)
    return lax.psum(kept, axis)


def kernel_values(left, right):
    products = lax.dot_general(
        left, right, (((1,), (1,)), ((), ())), preferred_element_type=jnp.float32
    )
    scaled = products * left.shape[1] ** (-0.5)
    squared = scaled * scaled
    return 0.25 * squared * squared


def live_weights(pool_count, pool_weight):
    members = jnp.arange(pool_weight.shape[1], dtype=jnp.int32)
    return jnp.where(members[None, :] < pool_count[:, None], pool_weight, 0.0)


def pool_rows(kernel_table, env_index, weights_live):
    pooled = jnp.zeros((env_index.shape[0], kernel_table.shape[1]), jnp.float32)
    for member in range(env_index.shape[1]):
        pooled = pooled + weights_live[:, member : member + 1] * kernel_table[env_index[:, member]]
    return pooled


def on_any_device(env_desc, point_desc, pool_index, pool_count, pool_weight, row_dest):
    groups = lax.axis_size("rows")
    slot_total = pool_index.shape[0]
    balanced = slot_total // 2
    slot_share = slot_total // groups
    points = lax.all_gather(point_desc, "rows", axis=1, tiled=True)
    width_pts = points.shape[0]
    weights_live = live_weights(pool_count, pool_weight)
    live_slot = row_dest >= 0
    owner_group = jnp.where(live_slot, row_dest // balanced, groups)
    within = jnp.where(live_slot, row_dest % balanced, balanced)
    owner_table = (owner_group[:, None] == jnp.arange(groups, dtype=jnp.int32)[None, :]).astype(
        jnp.int32
    )
    earlier = jnp.cumsum(owner_table, axis=0) - owner_table
    slot_rank = jnp.sum(earlier * owner_table, axis=1)
    outbox_place = (
        jnp.full((groups, slot_share), balanced, jnp.int32)
        .at[owner_group, slot_rank]
        .set(within, mode="drop")
    )
    features = lax.all_gather(env_desc, "pts", axis=1, tiled=True)
    slot_rows = pool_rows(kernel_values(features, points), pool_index, weights_live)
    outbox = (
        jnp.zeros((groups, slot_share, width_pts), jnp.float32)
        .at[owner_group, slot_rank]
        .set(slot_rows, mode="drop")
    )
    inbox_rows, inbox_place = (
        lax.all_to_all(outbox, "rows", split_axis=0, concat_axis=0, tiled=True),
        lax.all_to_all(outbox_place, "rows", split_axis=0, concat_axis=0, tiled=True),
    )
    design = (
        jnp.zeros((balanced, width_pts), jnp.float32)
        .at[inbox_place.reshape(-1)]
        .set(inbox_rows.reshape(-1, width_pts), mode="drop")
    )
    all_rows = lax.all_gather(design, "rows", axis=0, tiled=True)
    per_group = lax.axis_size("pts") // groups
    row_group = lax.axis_index("rows")
    pieces = []
    for part_index in range(per_group):
        diagonal_panel = from_root(all_rows, "pts", row_group * per_group + part_index)
        pieces.append(
            lax.dot_general(
                diagonal_panel,
                all_rows,
                (((0,), (0,)), ((), ())),
                precision=lax.Precision.HIGHEST,
                preferred_element_type=jnp.float32,
            )
        )
    gram_tile = jnp.concatenate(pieces, axis=0) * (1.0 / all_rows.shape[0])
    tile_rows = gram_tile.shape[0]
    row_ids = row_group * tile_rows + jnp.arange(tile_rows, dtype=jnp.int32)
    col_ids = lax.axis_index("pts") * width_pts + jnp.arange(width_pts, dtype=jnp.int32)
    gram_tile = gram_tile + jnp.where(row_ids[:, None] == col_ids[None, :], damping, 0.0)
    return (design, gram_tile)


def dot_nn(a, b):
    return lax.dot_general(a, b, (((1,), (0,)), ((), ())), preferred_element_type=F32)


def dot_nt(a, b):
    return lax.dot_general(a, b, (((1,), (1,)), ((), ())), preferred_element_type=F32)


def split(value):
    high = value.astype(BF16)
    return high, (value - high.astype(F32)).astype(BF16)


def encode(value, code_ref):
    n = value.shape[0]
    size = jnp.abs(value)
    top = jnp.maximum(jnp.max(size, axis=0, keepdims=True), 1e-30)
    exponent = jnp.ceil(jnp.log(top) * 1.4426950408889634)
    root = jnp.sqrt(size * jnp.exp2(-exponent))
    code = jnp.minimum(root * CODE_TOP + 0.5, 32767.0).astype(jnp.int32)
    code_ref[pl.ds(0, n), :] = jnp.where(value < 0, -code, code).astype(jnp.int16)
    pad = code_ref.shape[0] - n
    code_ref[pl.ds(n, pad), :] = jnp.broadcast_to(
        exponent.astype(jnp.int32), (pad, value.shape[1])
    ).astype(jnp.int16)


def lane_scale(exponent_rows, extra):
    exponent = exponent_rows.astype(jnp.int32).astype(F32)[0:1, :]
    return jnp.exp2(exponent) * (extra / (CODE_TOP * CODE_TOP))


def decode(codes, scale):
    root = codes.astype(jnp.int32).astype(F32)
    return root * jnp.abs(root) * scale


def weights_kernel(*refs):
    tables, high_ref, low_ref = refs[:-2], refs[-2], refs[-1]
    rows, envs = high_ref.shape[1:]
    for d, ref in enumerate(tables):
        lanes = ref.shape[1]
        piece = ref[...].astype(F32)
        piece = jnp.concatenate([piece[0:32], piece[32:64]], axis=1)
        slots = 2 * lanes
        index = piece[0:4] * 256.0 + piece[4:8]
        weight = piece[8:12] + piece[12:16] + piece[16:20]
        place = piece[20:21] * 256.0 + piece[21:22] - 1.0
        row_id = lax.broadcasted_iota(jnp.int32, (rows, slots), 0).astype(F32)
        by_row = lax.dot_general(
            jnp.where(place == row_id, 1.0, 0.0),
            jnp.concatenate([index, weight], axis=0),
            (((1,), (1,)), ((), ())),
            precision=lax.Precision.HIGHEST,
            preferred_element_type=F32,
        )
        env_id = lax.broadcasted_iota(jnp.int32, (rows, envs), 1).astype(F32)
        index = jnp.floor(by_row + 0.5)
        total = jnp.zeros((rows, envs), F32)
        for member in range(4):
            total = total + jnp.where(
                index[:, member : member + 1] == env_id, by_row[:, 4 + member : 5 + member], 0.0
            )
        high, low = split(total)
        high_ref[d] = high
        low_ref[d] = low


def fourth_power(products, scale):
    s = products * scale
    s = s * s
    return split(0.25 * s * s)


def add_columns(features, weights, pts, total, first):
    high, low = weights[0], weights[1]
    k_high, k_low = fourth_power(dot_nt(features, pts[...]), features.shape[1] ** (-0.5))
    part = dot_nn(high, k_high) + dot_nn(high, k_low) + dot_nn(low, k_high)
    total[...] = part if first else total[...] + part


def add_panel(features, weights, pts, total, first):
    high, low = weights[0], weights[1]
    k_high, k_low = fourth_power(dot_nt(pts[...], features), features.shape[1] ** (-0.5))
    part = dot_nt(k_high, high) + dot_nt(k_low, high) + dot_nt(k_high, low)
    total[...] = part if first else total[...] + part


def started(copies):
    for copy in copies:
        copy.start()
    return copies


def waited(copies):
    for copy in copies:
        copy.wait()


def group_copies(at_ref, d, sides, weights_from, env, weights, sems):
    z, core = at_ref[1], at_ref[2]
    envs, part = env.shape[0], sides[0][0].shape[1]
    out = []
    for side, refs in zip((core, 1 - core), sides):
        for r in range(4):
            at = pl.multiple_of((jnp.bitwise_xor(z, r) * 2 + side) * part, part)
            source = refs[d].at[pl.ds(r * envs, envs)]
            out.append(pltpu.make_async_copy(source, env.at[:, pl.ds(at, part)], sems.at[len(out)]))
    for i in range(2):
        source = weights_from[i].at[d] if d < 3 else weights_from[2 + i].at[0]
        out.append(pltpu.make_async_copy(source, weights.at[i], sems.at[8 + i]))
    return out


def design_kernel(at_ref, *refs):
    sides, cols, panels, weights_from = (refs[0:4], refs[4:8]), refs[8], refs[9:13], refs[13:17]
    cols_code, panel_code, rows_out = refs[17:20]
    cols_pts, panel_pts, env, weights, cols_sum, panel_sum, point_sems, group_sems = refs[20:]
    q, z = at_ref[0], at_ref[1]
    n_pts, comps = panels[0].shape
    points = []
    for j in range(4):
        to = cols_pts.at[:, pl.ds(j * comps, comps)]
        points.append(pltpu.make_async_copy(cols.at[j], to, point_sems.at[j]))
    started(points)
    copies = [
        group_copies(at_ref, d, sides, weights_from, env.at[d], weights.at[d], group_sems.at[d])
        for d in range(4)
    ]
    started(copies[0])
    panel = []
    for t, ref in enumerate(panels):
        at = pl.multiple_of(jnp.bitwise_xor(z, t) * comps, comps)
        to = panel_pts.at[:, pl.ds(at, comps)]
        panel.append(pltpu.make_async_copy(ref, to, point_sems.at[4 + t]))
    started(panel)
    for d in range(1, 4):
        started(copies[d])
    waited(points)
    for d in range(4):
        waited(copies[d])
        add_columns(env[d], weights.at[d], cols_pts, cols_sum, d == 0)
        if d == 0:
            waited(panel)
        add_panel(env[d], weights.at[d], panel_pts, panel_sum, d == 0)
    encode(cols_sum[...], cols_code)
    share = rows_out.shape[0]
    rows_out[...] = cols_sum[pl.ds(pl.multiple_of(q * share, share), share), :]
    encode(panel_sum[...], panel_code)


def value_pair(codes, scale, out):
    rows = out.shape[0] // 2
    high, low = split(decode(codes, scale))
    out[pl.ds(0, rows), :] = high
    out[pl.ds(rows, rows), :] = low


def near_columns_kernel(code0, code1, code2, out_ref):
    rows = out_ref.shape[1] // 2
    for d, ref in enumerate((code0, code1, code2)):

        @pl.when(pl.program_id(0) == d)
        def _():
            value_pair(ref[pl.ds(0, rows), :], lane_scale(ref[pl.ds(rows, 16), :], 1.0), out_ref.at[0])


def far_columns_kernel(at_ref, rows_ref, code1, code2, code3, out_ref, design_ref):
    q = at_ref[0]
    rows = out_ref.shape[1] // 2
    share, n_pts = rows_ref.shape
    value_pair(code3[pl.ds(0, rows), :], lane_scale(code3[pl.ds(rows, 16), :], 1.0), out_ref.at[0])
    start = pl.multiple_of(q * share, share)

    def put(d, value):
        at = pl.multiple_of(jnp.bitwise_xor(q, d) * n_pts, n_pts)
        design_ref[:, pl.ds(at, n_pts)] = value

    put(0, rows_ref[...])
    for d, ref in enumerate((code1, code2, code3), 1):
        put(d, decode(ref[pl.ds(start, share), :], lane_scale(ref[pl.ds(rows, 16), :], 1.0)))


def gray(value):
    return jnp.bitwise_xor(value, lax.shift_right_logical(value, 1))


def ring_source(z, steps):
    return gray(jnp.bitwise_and(gray(z) - steps, 3))


def gram_kernel(steps, first, n_near, at_ref, *refs):
    n_codes = 2 * len(steps)
    codes, value_refs, out_ref, left = refs[:n_codes], refs[n_codes:-2], refs[-2], refs[-1]
    n, j = pl.program_id(0), pl.program_id(1)
    k, z, core = at_ref[0], at_ref[1], at_ref[2]
    source = ring_source(z, steps[0] + n)
    n_pts = out_ref.shape[1]
    rows = codes[0].shape[1]
    for i in range(len(steps)):

        @pl.when((j == 0) & (n == i))
        def _():
            for ref, side in ((codes[2 * i], core), (codes[2 * i + 1], 1 - core)):
                scale = lane_scale(ref[pl.ds(n_pts, 16), :], 1.0 / rows)
                high, low = split(decode(ref[pl.ds(0, n_pts), :], scale))
                left[side, :, pl.ds(0, rows)] = high
                left[side, :, pl.ds(rows, rows)] = low

    def multiply(pair_ref):
        for side in range(2):
            high, low = left[side, :, pl.ds(0, rows)], left[side, :, pl.ds(rows, rows)]
            top, rest = pair_ref[0, pl.ds(0, rows), :], pair_ref[0, pl.ds(rows, rows), :]
            out_ref[side] = dot_nn(high, top) + dot_nn(low, top) + dot_nn(high, rest)

    if first == 0 and n_near < 4:
        multiply(value_refs[0])
    elif first == 3:
        multiply(value_refs[0])
    else:
        pl.when(j < 3)(lambda: multiply(value_refs[0]))
        pl.when(j == 3)(lambda: multiply(value_refs[1]))

    @pl.when((k == z) & (jnp.bitwise_xor(k, first + j) == source))
    def _():
        eye = lax.broadcasted_iota(jnp.int32, out_ref.shape[1:], 0) == lax.broadcasted_iota(
            jnp.int32, out_ref.shape[1:], 1
        )
        out_ref[core] = out_ref[core] + jnp.where(eye, damping, 0.0)


def cost(multiply_adds, nbytes):
    return pl.CostEstimate(flops=2 * multiply_adds, bytes_accessed=nbytes, transcendentals=0)


def whole(shape):
    return pl.BlockSpec(shape, lambda *_: (0,) * len(shape))


def on_device(env_desc, point_desc, pool_index, pool_count, pool_weight, row_dest):
    groups, planes = 4, 4
    q = lax.axis_index("rows")
    p = lax.axis_index("pts")
    z, core = p // 2, p % 2
    at = jnp.stack([q, z, core]).astype(jnp.int32)
    n_rows = pool_index.shape[0] * groups // 2
    envs, part = env_desc.shape
    n_pts = point_desc.shape[0] // planes
    comps = point_desc.shape[1]
    n_pool = pool_index.shape[1]
    pad = n_rows + 16

    def permutation(to):
        return [
            (r * 8 + s, to(r, s // 2, s % 2)[0] * 8 + to(r, s // 2, s % 2)[1] * 2 + to(r, s // 2, s % 2)[2])
            for r in range(groups)
            for s in range(planes * 2)
        ]

    def moved(value, to):
        return lax.ppermute(value, BOTH, permutation(to))

    along_x = lambda r, h, c: (r ^ 1, h, c)
    along_y = lambda r, h, c: (r ^ 2, h, c)
    to_core = lambda r, h, c: (r, h, 1 - c)
    ring = (1, 3, 0, 2)
    along_z = lambda r, h, c: (r, ring[h], c)


    quarters = point_desc.reshape(planes, n_pts, comps)
    cols_pts = lax.all_to_all(quarters, "rows", 0, 0, tiled=True)

    members = jnp.arange(n_pool, dtype=jnp.int32)
    live = jnp.where(members[None, :] < pool_count[:, None], pool_weight, 0.0).T
    live_high = lax.reduce_precision(live, 8, 7)
    rest = live - live_high
    rest_high = lax.reduce_precision(rest, 8, 7)
    place = row_dest[None, :] + 1
    index = pool_index.T
    table = jnp.concatenate(
        [
            (index // 256).astype(BF16),
            (index % 256).astype(BF16),
            live_high.astype(BF16),
            rest_high.astype(BF16),
            (rest - rest_high).astype(BF16),
            (place // 256).astype(BF16),
            (place % 256).astype(BF16),
            jnp.zeros((10, index.shape[1]), BF16),
        ],
        axis=0,
    )

    own = jnp.concatenate(
        [
            env_desc,
            *(moved(env_desc, lambda r, h, c, d=d: (r, h ^ d, c)) for d in (1, 2, 3)),
            table[:, :part],
            table[:, part:],
        ]
    )
    own, cols_pts, quarters, at = lax.optimization_barrier((own, cols_pts, quarters, at))
    near_x, near_y = moved(own, along_x), moved(own, along_y)
    swap_own = moved(own, to_core)

    panel_pts = [
        moved(
            lax.dynamic_index_in_dim(quarters, q ^ t, 0, keepdims=False),
            lambda r, h, c, t=t: (h, r ^ t, c),
        )
        for t in range(planes)
    ]

    def pool_weights(tables):
        n = len(tables)
        return pl.pallas_call(
            weights_kernel,
            grid=(1,),
            in_specs=[
                pl.BlockSpec((64, part), lambda _, last=t.shape[0] // 64 - 1: (last, 0))
                for t in tables
            ],
            out_specs=[whole((n, n_rows, envs))] * 2,
            out_shape=[jax.ShapeDtypeStruct((n, n_rows, envs), BF16)] * 2,
            compiler_params=pltpu.CompilerParams(vmem_limit_bytes=VMEM_LIMIT),
            cost_estimate=cost(n * n_rows * n_rows * 16 * 6, n * MIB),
            name="pool_weights",
        )(*tables)

    far = moved(near_y, along_x)
    near_weights = pool_weights([own, near_x, near_y])
    near_x, near_y, *near_weights = lax.optimization_barrier((near_x, near_y, *near_weights))
    swap_x, swap_y = moved(near_x, to_core), moved(near_y, to_core)
    far, *rest = lax.optimization_barrier((far, *near_weights, *panel_pts))
    near_weights, panel_pts = rest[:2], rest[2:]
    mine = (own, near_x, near_y, far)
    other = (swap_own, swap_x, swap_y, moved(far, to_core))
    weights = (*near_weights, *pool_weights([far]))

    anywhere = pl.BlockSpec(memory_space=pl.ANY)

    pts_scratch = pltpu.VMEM((n_pts, groups * comps), BF16)
    cols_code, panel_code, own_rows = pl.pallas_call(
        design_kernel,
        grid_spec=pltpu.PrefetchScalarGridSpec(
            num_scalar_prefetch=1,
            grid=(1,),
            in_specs=[anywhere] * 17,
            out_specs=[
                whole((pad, n_pts)),
                whole((n_pts + 16, n_rows)),
                whole((n_rows // groups, n_pts)),
            ],
            scratch_shapes=[
                pts_scratch,
                pts_scratch,
                pltpu.VMEM((groups, envs, groups * comps), BF16),
                pltpu.VMEM((groups, 2, n_rows, envs), BF16),
                pltpu.VMEM((n_rows, n_pts), F32),
                pltpu.VMEM((n_pts, n_rows), F32),
                pltpu.SemaphoreType.DMA((8,)),
                pltpu.SemaphoreType.DMA((4, 10)),
            ],
        ),
        out_shape=[
            jax.ShapeDtypeStruct((pad, n_pts), jnp.int16),
            jax.ShapeDtypeStruct((n_pts + 16, n_rows), jnp.int16),
            jax.ShapeDtypeStruct((n_rows // groups, n_pts), F32),
        ],
        compiler_params=pltpu.CompilerParams(vmem_limit_bytes=VMEM_LIMIT),
        cost_estimate=cost(8 * n_pts * envs * (groups * comps + 3 * n_rows), 14 * MIB),
        name="design_values",
    )(at, *mine, *other, cols_pts, *panel_pts, *weights)

    held = [panel_code, moved(panel_code, along_z)]
    from_x, from_y = moved(cols_code, along_x), moved(cols_code, along_y)
    swapped = [moved(panel_code, to_core)]
    from_far = moved(from_y, along_x)
    width = groups * n_pts
    code_spec = whole((pad, n_pts))
    near = pl.pallas_call(
        near_columns_kernel,
        grid=(3,),
        in_specs=[code_spec] * 3,
        out_specs=pl.BlockSpec((1, 2 * n_rows, n_pts), lambda d: (d, 0, 0)),
        out_shape=jax.ShapeDtypeStruct((3, 2 * n_rows, n_pts), BF16),
        compiler_params=pltpu.CompilerParams(vmem_limit_bytes=VMEM_LIMIT),
        cost_estimate=cost(0, 6 * MIB),
        name="near_columns",
    )(cols_code, from_x, from_y)
    far, design = pl.pallas_call(
        far_columns_kernel,
        grid_spec=pltpu.PrefetchScalarGridSpec(
            num_scalar_prefetch=1,
            grid=(1,),
            in_specs=[
                whole((n_rows // groups, n_pts)),
                code_spec,
                code_spec,
                code_spec,
            ],
            out_specs=[whole((1, 2 * n_rows, n_pts)), whole((n_rows // groups, width))],
        ),
        out_shape=[
            jax.ShapeDtypeStruct((1, 2 * n_rows, n_pts), BF16),
            jax.ShapeDtypeStruct((n_rows // groups, width), F32),
        ],
        compiler_params=pltpu.CompilerParams(vmem_limit_bytes=VMEM_LIMIT),
        cost_estimate=cost(0, 5 * MIB),
        name="far_columns",
    )(at, own_rows, from_x, from_y, from_far)

    panel_spec = whole((n_pts + 16, n_rows))

    def gram_rows(gram, steps, first, n_near):
        values, value_specs = [], []
        if first < 3:
            values.append(near)
            value_specs.append(
                pl.BlockSpec((1, 2 * n_rows, n_pts), lambda n, j, _: (jnp.minimum(j, 2), 0, 0))
            )
        if first + n_near == 4:
            values.append(far)
            value_specs.append(whole((1, 2 * n_rows, n_pts)))
        operands = [at, *(c for i in steps for c in (held[i], swapped[i])), *values]
        in_specs = [panel_spec] * (2 * len(steps)) + value_specs
        aliases = {}
        if gram is not None:
            aliases = {len(operands): 0}
            in_specs.append(anywhere)
            operands.append(gram)
        return pl.pallas_call(
            functools.partial(gram_kernel, steps, first, n_near),
            grid_spec=pltpu.PrefetchScalarGridSpec(
                num_scalar_prefetch=1,
                grid=(len(steps), n_near),
                in_specs=in_specs,
                out_specs=pl.BlockSpec(
                    (2, n_pts, n_pts),
                    lambda n, j, s: (0, ring_source(s[1], steps[0] + n), jnp.bitwise_xor(s[0], first + j)),
                ),
                scratch_shapes=[pltpu.VMEM((2, n_pts, 2 * n_rows), BF16)],
            ),
            out_shape=jax.ShapeDtypeStruct((2, planes * n_pts, width), F32),
            input_output_aliases=aliases,
            compiler_params=pltpu.CompilerParams(vmem_limit_bytes=VMEM_LIMIT),
            cost_estimate=cost(len(steps) * n_near * 8 * n_pts * n_pts * n_rows, 4 * MIB),
            name="gram_rows",
        )(*operands)

    held.append(moved(held[1], along_z))
    swapped.append(moved(held[1], to_core))
    gram = gram_rows(None, (0, 1), 0, 3)
    held[2], gram = lax.optimization_barrier((held[2], gram))
    held.append(moved(held[2], along_z))
    swapped.append(moved(held[2], to_core))
    gram = gram_rows(gram, (0, 1), 3, 1)
    held[3], gram = lax.optimization_barrier((held[3], gram))
    swapped.append(moved(held[3], to_core))
    gram = gram_rows(gram, (2,), 0, 4)
    gram = gram_rows(gram, (3,), 0, 4)
    return design, gram.reshape(2 * planes * n_pts, width)


def solution(mesh):
    in_specs = (
        P("rows", "pts"),
        P("pts", "rows"),
        P("rows", None),
        P("rows"),
        P("rows", None),
        P("rows"),
    )
    out_specs = (P("rows", "pts"), P("rows", "pts"))
    body = on_device if dict(mesh.shape) == {"rows": 4, "pts": 8} else on_any_device
    return jax.shard_map(body, mesh=mesh, in_specs=in_specs, out_specs=out_specs, check_vma=False)
```

```python
import functools

import jax
import jax.numpy as jnp
from jax import lax
from jax.experimental import pallas as pl
from jax.experimental.pallas import tpu as pltpu
from jax.sharding import PartitionSpec as P

damping = 0.5
CODE_TOP = 32700.0
BOTH = ("rows", "pts")
MIB = 1 << 20
VMEM_LIMIT = 63 * MIB
F32 = jnp.float32
BF16 = jnp.bfloat16


def from_root(value, axis, source):
    kept = jnp.where(lax.axis_index(axis) == source, value, 0).astype(value.dtype)
    return lax.psum(kept, axis)


def kernel_values(left, right):
    products = lax.dot_general(
        left, right, (((1,), (1,)), ((), ())), preferred_element_type=jnp.float32
    )
    scaled = products * left.shape[1] ** (-0.5)
    squared = scaled * scaled
    return 0.25 * squared * squared


def live_weights(pool_count, pool_weight):
    members = jnp.arange(pool_weight.shape[1], dtype=jnp.int32)
    return jnp.where(members[None, :] < pool_count[:, None], pool_weight, 0.0)


def pool_rows(kernel_table, env_index, weights_live):
    pooled = jnp.zeros((env_index.shape[0], kernel_table.shape[1]), jnp.float32)
    for member in range(env_index.shape[1]):
        pooled = pooled + weights_live[:, member : member + 1] * kernel_table[env_index[:, member]]
    return pooled


def on_any_device(env_desc, point_desc, pool_index, pool_count, pool_weight, row_dest):
    groups = lax.axis_size("rows")
    slot_total = pool_index.shape[0]
    balanced = slot_total // 2
    slot_share = slot_total // groups
    points = lax.all_gather(point_desc, "rows", axis=1, tiled=True)
    width_pts = points.shape[0]
    weights_live = live_weights(pool_count, pool_weight)
    live_slot = row_dest >= 0
    owner_group = jnp.where(live_slot, row_dest // balanced, groups)
    within = jnp.where(live_slot, row_dest % balanced, balanced)
    owner_table = (owner_group[:, None] == jnp.arange(groups, dtype=jnp.int32)[None, :]).astype(
        jnp.int32
    )
    earlier = jnp.cumsum(owner_table, axis=0) - owner_table
    slot_rank = jnp.sum(earlier * owner_table, axis=1)
    outbox_place = (
        jnp.full((groups, slot_share), balanced, jnp.int32)
        .at[owner_group, slot_rank]
        .set(within, mode="drop")
    )
    features = lax.all_gather(env_desc, "pts", axis=1, tiled=True)
    slot_rows = pool_rows(kernel_values(features, points), pool_index, weights_live)
    outbox = (
        jnp.zeros((groups, slot_share, width_pts), jnp.float32)
        .at[owner_group, slot_rank]
        .set(slot_rows, mode="drop")
    )
    inbox_rows, inbox_place = (
        lax.all_to_all(outbox, "rows", split_axis=0, concat_axis=0, tiled=True),
        lax.all_to_all(outbox_place, "rows", split_axis=0, concat_axis=0, tiled=True),
    )
    design = (
        jnp.zeros((balanced, width_pts), jnp.float32)
        .at[inbox_place.reshape(-1)]
        .set(inbox_rows.reshape(-1, width_pts), mode="drop")
    )
    all_rows = lax.all_gather(design, "rows", axis=0, tiled=True)
    per_group = lax.axis_size("pts") // groups
    row_group = lax.axis_index("rows")
    pieces = []
    for part_index in range(per_group):
        diagonal_panel = from_root(all_rows, "pts", row_group * per_group + part_index)
        pieces.append(
            lax.dot_general(
                diagonal_panel,
                all_rows,
                (((0,), (0,)), ((), ())),
                precision=lax.Precision.HIGHEST,
                preferred_element_type=jnp.float32,
            )
        )
    gram_tile = jnp.concatenate(pieces, axis=0) * (1.0 / all_rows.shape[0])
    tile_rows = gram_tile.shape[0]
    row_ids = row_group * tile_rows + jnp.arange(tile_rows, dtype=jnp.int32)
    col_ids = lax.axis_index("pts") * width_pts + jnp.arange(width_pts, dtype=jnp.int32)
    gram_tile = gram_tile + jnp.where(row_ids[:, None] == col_ids[None, :], damping, 0.0)
    return (design, gram_tile)


def dot_nn(a, b):
    return lax.dot_general(a, b, (((1,), (0,)), ((), ())), preferred_element_type=F32)


def dot_nt(a, b):
    return lax.dot_general(a, b, (((1,), (1,)), ((), ())), preferred_element_type=F32)


def split(value):
    high = value.astype(BF16)
    return high, (value - high.astype(F32)).astype(BF16)


def encode(value, code_ref):
    n = value.shape[0]
    size = jnp.abs(value)
    top = jnp.maximum(jnp.max(size, axis=0, keepdims=True), 1e-30)
    exponent = jnp.ceil(jnp.log(top) * 1.4426950408889634)
    root = jnp.sqrt(size * jnp.exp2(-exponent))
    code = jnp.minimum(root * CODE_TOP + 0.5, 32767.0).astype(jnp.int32)
    code_ref[pl.ds(0, n), :] = jnp.where(value < 0, -code, code).astype(jnp.int16)
    pad = code_ref.shape[0] - n
    code_ref[pl.ds(n, pad), :] = jnp.broadcast_to(
        exponent.astype(jnp.int32), (pad, value.shape[1])
    ).astype(jnp.int16)


def lane_scale(exponent_rows, extra):
    exponent = exponent_rows.astype(jnp.int32).astype(F32)[0:1, :]
    return jnp.exp2(exponent) * (extra / (CODE_TOP * CODE_TOP))


def decode(codes, scale):
    root = codes.astype(jnp.int32).astype(F32)
    return root * jnp.abs(root) * scale


def weights_kernel(*refs):
    tables, high_ref, low_ref = refs[:-2], refs[-2], refs[-1]
    rows, envs = high_ref.shape[1:]
    for d, ref in enumerate(tables):
        lanes = ref.shape[1]
        piece = ref[...].astype(F32)
        piece = jnp.concatenate([piece[0:32], piece[32:64]], axis=1)
        slots = 2 * lanes
        index = piece[0:4] * 256.0 + piece[4:8]
        weight = piece[8:12] + piece[12:16] + piece[16:20]
        place = piece[20:21] * 256.0 + piece[21:22] - 1.0
        row_id = lax.broadcasted_iota(jnp.int32, (rows, slots), 0).astype(F32)
        by_row = lax.dot_general(
            jnp.where(place == row_id, 1.0, 0.0),
            jnp.concatenate([index, weight], axis=0),
            (((1,), (1,)), ((), ())),
            precision=lax.Precision.HIGHEST,
            preferred_element_type=F32,
        )
        env_id = lax.broadcasted_iota(jnp.int32, (rows, envs), 1).astype(F32)
        index = jnp.floor(by_row + 0.5)
        total = jnp.zeros((rows, envs), F32)
        for member in range(4):
            total = total + jnp.where(
                index[:, member : member + 1] == env_id, by_row[:, 4 + member : 5 + member], 0.0
            )
        high, low = split(total)
        high_ref[d] = high
        low_ref[d] = low


def fourth_power(products, scale):
    s = products * scale
    s = s * s
    return split(0.25 * s * s)


def add_columns(features, weights, pts, total, first):
    high, low = weights[0], weights[1]
    k_high, k_low = fourth_power(dot_nt(features, pts[...]), features.shape[1] ** (-0.5))
    part = dot_nn(high, k_high) + dot_nn(high, k_low) + dot_nn(low, k_high)
    total[...] = part if first else total[...] + part


def add_panel(features, weights, pts, total, first):
    high, low = weights[0], weights[1]
    k_high, k_low = fourth_power(dot_nt(pts[...], features), features.shape[1] ** (-0.5))
    part = dot_nt(k_high, high) + dot_nt(k_low, high) + dot_nt(k_high, low)
    total[...] = part if first else total[...] + part


def started(copies):
    for copy in copies:
        copy.start()
    return copies


def waited(copies):
    for copy in copies:
        copy.wait()


def group_copies(at_ref, d, sides, weights_from, env, weights, sems):
    z, core = at_ref[1], at_ref[2]
    envs, part = env.shape[0], sides[0][0].shape[1]
    out = []
    for side, refs in zip((core, 1 - core), sides):
        for r in range(4):
            at = pl.multiple_of((jnp.bitwise_xor(z, r) * 2 + side) * part, part)
            source = refs[d].at[pl.ds(r * envs, envs)]
            out.append(pltpu.make_async_copy(source, env.at[:, pl.ds(at, part)], sems.at[len(out)]))
    for i in range(2):
        source = weights_from[i].at[d] if d < 3 else weights_from[2 + i].at[0]
        out.append(pltpu.make_async_copy(source, weights.at[i], sems.at[8 + i]))
    return out


def design_kernel(at_ref, *refs):
    sides, cols, panels, weights_from = (refs[0:4], refs[4:8]), refs[8], refs[9:13], refs[13:17]
    cols_code, panel_code, rows_out = refs[17:20]
    cols_pts, panel_pts, env, weights, cols_sum, panel_sum, point_sems, group_sems = refs[20:]
    q, z = at_ref[0], at_ref[1]
    n_pts, comps = panels[0].shape
    points = []
    for j in range(4):
        to = cols_pts.at[:, pl.ds(j * comps, comps)]
        points.append(pltpu.make_async_copy(cols.at[j], to, point_sems.at[j]))
    started(points)
    copies = [
        group_copies(at_ref, d, sides, weights_from, env.at[d], weights.at[d], group_sems.at[d])
        for d in range(4)
    ]
    started(copies[0])
    panel = []
    for t, ref in enumerate(panels):
        at = pl.multiple_of(jnp.bitwise_xor(z, t) * comps, comps)
        to = panel_pts.at[:, pl.ds(at, comps)]
        panel.append(pltpu.make_async_copy(ref, to, point_sems.at[4 + t]))
    started(panel)
    for d in range(1, 4):
        started(copies[d])
    waited(points)
    for d in range(4):
        waited(copies[d])
        add_columns(env[d], weights.at[d], cols_pts, cols_sum, d == 0)
        if d == 0:
            waited(panel)
        add_panel(env[d], weights.at[d], panel_pts, panel_sum, d == 0)
    encode(cols_sum[...], cols_code)
    share = rows_out.shape[0]
    rows_out[...] = cols_sum[pl.ds(pl.multiple_of(q * share, share), share), :]
    encode(panel_sum[...], panel_code)


def value_pair(codes, scale, out):
    rows = out.shape[0] // 2
    high, low = split(decode(codes, scale))
    out[pl.ds(0, rows), :] = high
    out[pl.ds(rows, rows), :] = low


def near_columns_kernel(code0, code1, code2, out_ref):
    rows = out_ref.shape[1] // 2
    for d, ref in enumerate((code0, code1, code2)):

        @pl.when(pl.program_id(0) == d)
        def _():
            value_pair(ref[pl.ds(0, rows), :], lane_scale(ref[pl.ds(rows, 16), :], 1.0), out_ref.at[0])


def far_columns_kernel(at_ref, rows_ref, code1, code2, code3, out_ref, design_ref):
    q = at_ref[0]
    rows = out_ref.shape[1] // 2
    share, n_pts = rows_ref.shape
    value_pair(code3[pl.ds(0, rows), :], lane_scale(code3[pl.ds(rows, 16), :], 1.0), out_ref.at[0])
    start = pl.multiple_of(q * share, share)

    def put(d, value):
        at = pl.multiple_of(jnp.bitwise_xor(q, d) * n_pts, n_pts)
        design_ref[:, pl.ds(at, n_pts)] = value

    put(0, rows_ref[...])
    for d, ref in enumerate((code1, code2, code3), 1):
        put(d, decode(ref[pl.ds(start, share), :], lane_scale(ref[pl.ds(rows, 16), :], 1.0)))


def gray(value):
    return jnp.bitwise_xor(value, lax.shift_right_logical(value, 1))


def ring_source(z, steps):
    return gray(jnp.bitwise_and(gray(z) - steps, 3))


def gram_kernel(steps, first, n_near, at_ref, *refs):
    n_codes = 2 * len(steps)
    codes, value_refs, out_ref, left = refs[:n_codes], refs[n_codes:-2], refs[-2], refs[-1]
    n, j = pl.program_id(0), pl.program_id(1)
    k, z, core = at_ref[0], at_ref[1], at_ref[2]
    source = ring_source(z, steps[0] + n)
    n_pts = out_ref.shape[1]
    rows = codes[0].shape[1]
    for i in range(len(steps)):

        @pl.when((j == 0) & (n == i))
        def _():
            for ref, side in ((codes[2 * i], core), (codes[2 * i + 1], 1 - core)):
                scale = lane_scale(ref[pl.ds(n_pts, 16), :], 1.0 / rows)
                high, low = split(decode(ref[pl.ds(0, n_pts), :], scale))
                left[side, :, pl.ds(0, rows)] = high
                left[side, :, pl.ds(rows, rows)] = low

    def multiply(pair_ref):
        for side in range(2):
            high, low = left[side, :, pl.ds(0, rows)], left[side, :, pl.ds(rows, rows)]
            top, rest = pair_ref[0, pl.ds(0, rows), :], pair_ref[0, pl.ds(rows, rows), :]
            out_ref[side] = dot_nn(high, top) + dot_nn(low, top) + dot_nn(high, rest)

    if first == 0 and n_near < 4:
        multiply(value_refs[0])
    elif first == 3:
        multiply(value_refs[0])
    else:
        pl.when(j < 3)(lambda: multiply(value_refs[0]))
        pl.when(j == 3)(lambda: multiply(value_refs[1]))

    @pl.when((k == z) & (jnp.bitwise_xor(k, first + j) == source))
    def _():
        eye = lax.broadcasted_iota(jnp.int32, out_ref.shape[1:], 0) == lax.broadcasted_iota(
            jnp.int32, out_ref.shape[1:], 1
        )
        out_ref[core] = out_ref[core] + jnp.where(eye, damping, 0.0)


def cost(multiply_adds, nbytes):
    return pl.CostEstimate(flops=2 * multiply_adds, bytes_accessed=nbytes, transcendentals=0)


def whole(shape):
    return pl.BlockSpec(shape, lambda *_: (0,) * len(shape))


def on_device(env_desc, point_desc, pool_index, pool_count, pool_weight, row_dest):
    groups, planes = 4, 4
    q = lax.axis_index("rows")
    p = lax.axis_index("pts")
    z, core = p // 2, p % 2
    at = jnp.stack([q, z, core]).astype(jnp.int32)
    n_rows = pool_index.shape[0] * groups // 2
    envs, part = env_desc.shape
    n_pts = point_desc.shape[0] // planes
    comps = point_desc.shape[1]
    n_pool = pool_index.shape[1]
    pad = n_rows + 16

    def permutation(to):
        return [
            (r * 8 + s, to(r, s // 2, s % 2)[0] * 8 + to(r, s // 2, s % 2)[1] * 2 + to(r, s // 2, s % 2)[2])
            for r in range(groups)
            for s in range(planes * 2)
        ]

    def moved(value, to):
        return lax.ppermute(value, BOTH, permutation(to))

    along_x = lambda r, h, c: (r ^ 1, h, c)
    along_y = lambda r, h, c: (r ^ 2, h, c)
    to_core = lambda r, h, c: (r, h, 1 - c)
    ring = (1, 3, 0, 2)
    along_z = lambda r, h, c: (r, ring[h], c)


    quarters = point_desc.reshape(planes, n_pts, comps)
    cols_pts = lax.all_to_all(quarters, "rows", 0, 0, tiled=True)

    members = jnp.arange(n_pool, dtype=jnp.int32)
    live = jnp.where(members[None, :] < pool_count[:, None], pool_weight, 0.0).T
    live_high = lax.reduce_precision(live, 8, 7)
    rest = live - live_high
    rest_high = lax.reduce_precision(rest, 8, 7)
    place = row_dest[None, :] + 1
    index = pool_index.T
    table = jnp.concatenate(
        [
            (index // 256).astype(BF16),
            (index % 256).astype(BF16),
            live_high.astype(BF16),
            rest_high.astype(BF16),
            (rest - rest_high).astype(BF16),
            (place // 256).astype(BF16),
            (place % 256).astype(BF16),
            jnp.zeros((10, index.shape[1]), BF16),
        ],
        axis=0,
    )

    own = jnp.concatenate(
        [
            env_desc,
            *(moved(env_desc, lambda r, h, c, d=d: (r, h ^ d, c)) for d in (1, 2, 3)),
            table[:, :part],
            table[:, part:],
        ]
    )
    own, cols_pts, quarters, at = lax.optimization_barrier((own, cols_pts, quarters, at))
    near_x, near_y = moved(own, along_x), moved(own, along_y)
    swap_own = moved(own, to_core)

    panel_pts = [
        moved(
            lax.dynamic_index_in_dim(quarters, q ^ t, 0, keepdims=False),
            lambda r, h, c, t=t: (h, r ^ t, c),
        )
        for t in range(planes)
    ]

    def pool_weights(tables):
        n = len(tables)
        return pl.pallas_call(
            weights_kernel,
            grid=(1,),
            in_specs=[
                pl.BlockSpec((64, part), lambda _, last=t.shape[0] // 64 - 1: (last, 0))
                for t in tables
            ],
            out_specs=[whole((n, n_rows, envs))] * 2,
            out_shape=[jax.ShapeDtypeStruct((n, n_rows, envs), BF16)] * 2,
            compiler_params=pltpu.CompilerParams(vmem_limit_bytes=VMEM_LIMIT),
            cost_estimate=cost(n * n_rows * n_rows * 16 * 6, n * MIB),
            name="pool_weights",
        )(*tables)

    far = moved(near_y, along_x)
    near_weights = pool_weights([own, near_x, near_y])
    near_x, near_y, *near_weights = lax.optimization_barrier((near_x, near_y, *near_weights))
    swap_x, swap_y = moved(near_x, to_core), moved(near_y, to_core)
    far, *rest = lax.optimization_barrier((far, *near_weights, *panel_pts))
    near_weights, panel_pts = rest[:2], rest[2:]
    mine = (own, near_x, near_y, far)
    other = (swap_own, swap_x, swap_y, moved(far, to_core))
    weights = (*near_weights, *pool_weights([far]))

    anywhere = pl.BlockSpec(memory_space=pl.ANY)

    pts_scratch = pltpu.VMEM((n_pts, groups * comps), BF16)
    cols_code, panel_code, own_rows = pl.pallas_call(
        design_kernel,
        grid_spec=pltpu.PrefetchScalarGridSpec(
            num_scalar_prefetch=1,
            grid=(1,),
            in_specs=[anywhere] * 17,
            out_specs=[
                whole((pad, n_pts)),
                whole((n_pts + 16, n_rows)),
                whole((n_rows // groups, n_pts)),
            ],
            scratch_shapes=[
                pts_scratch,
                pts_scratch,
                pltpu.VMEM((groups, envs, groups * comps), BF16),
                pltpu.VMEM((groups, 2, n_rows, envs), BF16),
                pltpu.VMEM((n_rows, n_pts), F32),
                pltpu.VMEM((n_pts, n_rows), F32),
                pltpu.SemaphoreType.DMA((8,)),
                pltpu.SemaphoreType.DMA((4, 10)),
            ],
        ),
        out_shape=[
            jax.ShapeDtypeStruct((pad, n_pts), jnp.int16),
            jax.ShapeDtypeStruct((n_pts + 16, n_rows), jnp.int16),
            jax.ShapeDtypeStruct((n_rows // groups, n_pts), F32),
        ],
        compiler_params=pltpu.CompilerParams(vmem_limit_bytes=VMEM_LIMIT),
        cost_estimate=cost(8 * n_pts * envs * (groups * comps + 3 * n_rows), 14 * MIB),
        name="design_values",
    )(at, *mine, *other, cols_pts, *panel_pts, *weights)

    held = [panel_code, moved(panel_code, along_z)]
    from_x, from_y = moved(cols_code, along_x), moved(cols_code, along_y)
    swapped = [moved(panel_code, to_core)]
    from_far = moved(from_y, along_x)
    width = groups * n_pts
    code_spec = whole((pad, n_pts))
    near = pl.pallas_call(
        near_columns_kernel,
        grid=(3,),
        in_specs=[code_spec] * 3,
        out_specs=pl.BlockSpec((1, 2 * n_rows, n_pts), lambda d: (d, 0, 0)),
        out_shape=jax.ShapeDtypeStruct((3, 2 * n_rows, n_pts), BF16),
        compiler_params=pltpu.CompilerParams(vmem_limit_bytes=VMEM_LIMIT),
        cost_estimate=cost(0, 6 * MIB),
        name="near_columns",
    )(cols_code, from_x, from_y)
    far, design = pl.pallas_call(
        far_columns_kernel,
        grid_spec=pltpu.PrefetchScalarGridSpec(
            num_scalar_prefetch=1,
            grid=(1,),
            in_specs=[
                whole((n_rows // groups, n_pts)),
                code_spec,
                code_spec,
                code_spec,
            ],
            out_specs=[whole((1, 2 * n_rows, n_pts)), whole((n_rows // groups, width))],
        ),
        out_shape=[
            jax.ShapeDtypeStruct((1, 2 * n_rows, n_pts), BF16),
            jax.ShapeDtypeStruct((n_rows // groups, width), F32),
        ],
        compiler_params=pltpu.CompilerParams(vmem_limit_bytes=VMEM_LIMIT),
        cost_estimate=cost(0, 5 * MIB),
        name="far_columns",
    )(at, own_rows, from_x, from_y, from_far)

    panel_spec = whole((n_pts + 16, n_rows))

    def gram_rows(gram, steps, first, n_near):
        values, value_specs = [], []
        if first < 3:
            values.append(near)
            value_specs.append(
                pl.BlockSpec((1, 2 * n_rows, n_pts), lambda n, j, _: (jnp.minimum(j, 2), 0, 0))
            )
        if first + n_near == 4:
            values.append(far)
            value_specs.append(whole((1, 2 * n_rows, n_pts)))
        operands = [at, *(c for i in steps for c in (held[i], swapped[i])), *values]
        in_specs = [panel_spec] * (2 * len(steps)) + value_specs
        aliases = {}
        if gram is not None:
            aliases = {len(operands): 0}
            in_specs.append(anywhere)
            operands.append(gram)
        return pl.pallas_call(
            functools.partial(gram_kernel, steps, first, n_near),
            grid_spec=pltpu.PrefetchScalarGridSpec(
                num_scalar_prefetch=1,
                grid=(len(steps), n_near),
                in_specs=in_specs,
                out_specs=pl.BlockSpec(
                    (2, n_pts, n_pts),
                    lambda n, j, s: (0, ring_source(s[1], steps[0] + n), jnp.bitwise_xor(s[0], first + j)),
                ),
                scratch_shapes=[pltpu.VMEM((2, n_pts, 2 * n_rows), BF16)],
            ),
            out_shape=jax.ShapeDtypeStruct((2, planes * n_pts, width), F32),
            input_output_aliases=aliases,
            compiler_params=pltpu.CompilerParams(vmem_limit_bytes=VMEM_LIMIT),
            cost_estimate=cost(len(steps) * n_near * 8 * n_pts * n_pts * n_rows, 4 * MIB),
            name="gram_rows",
        )(*operands)

    held.append(moved(held[1], along_z))
    swapped.append(moved(held[1], to_core))
    gram = gram_rows(None, (0, 1), 0, 3)
    held[2], gram = lax.optimization_barrier((held[2], gram))
    held.append(moved(held[2], along_z))
    swapped.append(moved(held[2], to_core))
    gram = gram_rows(gram, (0, 1), 3, 1)
    held[3], gram = lax.optimization_barrier((held[3], gram))
    swapped.append(moved(held[3], to_core))
    gram = gram_rows(gram, (2, 3), 0, 4)
    return design, gram.reshape(2 * planes * n_pts, width)


def solution(mesh):
    in_specs = (
        P("rows", "pts"),
        P("pts", "rows"),
        P("rows", None),
        P("rows"),
        P("rows", None),
        P("rows"),
    )
    out_specs = (P("rows", "pts"), P("rows", "pts"))
    body = on_device if dict(mesh.shape) == {"rows": 4, "pts": 8} else on_any_device
    return jax.shard_map(body, mesh=mesh, in_specs=in_specs, out_specs=out_specs, check_vma=False)
```
